128 devices in a mesh: clip: 64 (over y, z_lo, x, core), frame: 2 (over z_hi).
Axes of the slice: x: 4, y: 4, z: 4 (z_hi: 2, z_lo: 2; z = z_hi * 2 + z_lo), core: 2. Of those that a mesh axis runs over, the one named last changes fastest.
Arguments:
- tokens: bfloat16 [64, 8, 324, 384], P('clip', 'frame'), may hold values from -6 to 6
- attn_gain: float32 [384], replicated, may hold values from 0.25 to 1.75
- attn_shift: float32 [384], replicated, may hold values from -3 to 3
- w_qkv: bfloat16 [384, 1152], replicated, may hold values from -0.3125 to 0.3125
- query_bias: bfloat16 [384], replicated, may hold values from -4 to 4
- value_bias: bfloat16 [384], replicated, may hold values from -4 to 4
- w_proj: bfloat16 [384, 384], replicated, may hold values from -2.5 to 2.5
- proj_bias: bfloat16 [384], replicated, may hold values from -4 to 4
- mlp_gain: float32 [384], replicated, may hold values from 0.25 to 1.75
- mlp_shift: float32 [384], replicated, may hold values from -3 to 3
- w_expand: bfloat16 [384, 1536], replicated, may hold values from -0.3125 to 0.3125
- expand_bias: bfloat16 [1536], replicated, may hold values from -4 to 4
- w_reduce: bfloat16 [1536, 384], replicated, may hold values from -0.15625 to 0.15625
- reduce_bias: bfloat16 [384], replicated, may hold values from -4 to 4
- cotangent: bfloat16 [64, 8, 324, 384], P('clip', 'frame'), may hold values from -6 to 6
- resolution: int32 [64], P('clip'), may hold values from 100 to 324, as said below
- frame_count: int32 [64], P('clip'), may hold values from 5 to 8, as said below
Outputs:
- activations: bfloat16 [64, 8, 324, 384], P('clip', 'frame')
- grad_tokens: float32 [64, 8, 324, 384], P('clip', 'frame')
- grad_attn_gain: float32 [384], replicated
- grad_attn_shift: float32 [384], replicated
- grad_w_qkv: float32 [384, 1152], replicated
- grad_query_bias: float32 [384], replicated
- grad_value_bias: float32 [384], replicated
- grad_w_proj: float32 [384, 384], replicated
- grad_proj_bias: float32 [384], replicated
- grad_mlp_gain: float32 [384], replicated
- grad_mlp_shift: float32 [384], replicated
- grad_w_expand: float32 [384, 1536], replicated
- grad_expand_bias: float32 [1536], replicated
- grad_w_reduce: float32 [1536, 384], replicated
- grad_reduce_bias: float32 [384], replicated
- grad_norm: float32 [], replicated
The draws below stay inside these ranges and needn't reach their ends.
Inputs may be any that keep to these rules, and one draw needn't show every extreme that they name: `resolution`: each clip's value is one of 324 * 100 // 324, 324 * 196 // 324 and 324; some clip has 324. `frame_count`: some clip has all 8 frames live.
All inputs are finite; a program needn't handle non-finite values.
Results may differ from the reference program's by a relative error of at most 0.012.
Values may be sent and summed in bfloat16 or wider, within the bound.
A program may use at most 256 MiB of HBM per device.

```python
import jax
import jax.numpy as jnp
from jax import lax

D = 384
HEADS = 6
FF = 1536
FRAMES = 8
FRAME_CAP = 324
CLIPS = 64


def draw_resolution(key, part):
    key = jax.random.fold_in(key, 11)
    picks = jax.random.randint(key, (CLIPS,), 0, 4)
    table = jnp.array([FRAME_CAP * 100 // 324, FRAME_CAP * 196 // 324, FRAME_CAP, FRAME_CAP], dtype=jnp.int32)
    counts = table[picks]
    forced = jax.random.randint(jax.random.fold_in(key, 5), (), 0, CLIPS)
    return counts.at[forced].set(FRAME_CAP).astype(jnp.int32)


def draw_frame_count(key, part):
    key = jax.random.fold_in(key, 23)
    counts = jax.random.randint(key, (CLIPS,), FRAMES // 2 + 1, FRAMES + 1)
    forced = jax.random.randint(jax.random.fold_in(key, 9), (), 0, CLIPS)
    return counts.at[forced].set(FRAMES).astype(jnp.int32)


def block_levels(key, extent, cuts, least, top_value):
    def one(dim, blocks):
        heights = jax.random.uniform(jax.random.fold_in(jax.random.fold_in(key, 6), dim), (blocks,), jnp.float32, least / len(cuts), top_value / len(cuts))
        return jnp.repeat(jnp.exp(heights), extent[dim] // blocks).reshape((-1,) + (1,) * (len(extent) - dim - 1))

    level = one(*cuts[0])
    for cut in cuts[1:]:
        level = level * one(*cut)
    return level


def scatter_about(key, dims, deviation, bound, split=(), held_as=jnp.bfloat16):
    drawn = deviation * jax.random.normal(key, dims, jnp.float32)
    if split:
        drawn = drawn * block_levels(key, dims, split, -0.22, 0.18)
    return jnp.clip(drawn, -bound, bound).astype(held_as)


def setup_inputs(seed: int = 0) -> dict:
    streams_of = jax.random.split(jax.random.key(seed), 18)
    tokens = scatter_about(streams_of[0], (CLIPS, FRAMES, FRAME_CAP, D), 1.0, 6.0, ((0, 64), (1, 2)))
    attn_gain = jnp.clip(1.0 + 0.15 * jax.random.normal(streams_of[1], (D,), jnp.float32), 0.25, 1.75)
    attn_shift = scatter_about(streams_of[2], (D,), 0.3, 3.0, (), jnp.float32)
    w_qkv = scatter_about(streams_of[3], (D, 3 * D), D ** -0.5, 0.3125)
    query_bias = scatter_about(streams_of[4], (D,), 0.5, 4.0)
    value_bias = scatter_about(streams_of[5], (D,), 0.5, 4.0)
    w_proj = scatter_about(streams_of[6], (D, D), 6 ** -0.5, 2.5)
    proj_bias = scatter_about(streams_of[7], (D,), 0.5, 4.0)
    mlp_gain = jnp.clip(1.0 + 0.15 * jax.random.normal(streams_of[8], (D,), jnp.float32), 0.25, 1.75)
    mlp_shift = scatter_about(streams_of[9], (D,), 0.3, 3.0, (), jnp.float32)
    w_expand = scatter_about(streams_of[10], (D, FF), D ** -0.5, 0.3125)
    expand_bias = scatter_about(streams_of[11], (FF,), 0.5, 4.0)
    w_reduce = scatter_about(streams_of[12], (FF, D), FF ** -0.5, 0.15625)
    reduce_bias = scatter_about(streams_of[13], (D,), 0.5, 4.0)
    cotangent = scatter_about(streams_of[14], (CLIPS, FRAMES, FRAME_CAP, D), 1.0, 6.0, ((0, 64), (1, 2)))
    resolution = draw_resolution(jax.random.fold_in(streams_of[17], 71), 0)
    frame_count = draw_frame_count(jax.random.fold_in(streams_of[17], 71), 0)
    return dict(tokens=tokens, attn_gain=attn_gain, attn_shift=attn_shift, w_qkv=w_qkv, query_bias=query_bias, value_bias=value_bias, w_proj=w_proj, proj_bias=proj_bias, mlp_gain=mlp_gain, mlp_shift=mlp_shift, w_expand=w_expand, expand_bias=expand_bias, w_reduce=w_reduce, reduce_bias=reduce_bias, cotangent=cotangent, resolution=resolution, frame_count=frame_count)


EPS = 1e-06
SCALE = 0.125
highest = lax.Precision.HIGHEST

@jax.custom_vjp
def low(v):
    return lax.optimization_barrier(v.astype(jnp.bfloat16)).astype(jnp.float32)

@jax.custom_vjp
def low_back(v):
    return v

def low_keep(v):
    return (low(v), None)

def low_pass(kept, grad):
    return (grad,)

def back_keep(v):
    return (v, None)

def back_low(kept, grad):
    return (low(grad),)
low.defvjp(low_keep, low_pass)
low_back.defvjp(back_keep, back_low)

def layer_norm(values, scale_vector, shift_vector):
    centre = values - lax.optimization_barrier(jnp.mean(values, axis=-1, keepdims=True))
    spread = lax.optimization_barrier(jnp.mean(centre * centre, axis=-1, keepdims=True))
    return centre * lax.rsqrt(spread + EPS) * scale_vector + shift_vector

def windows(stacked):
    frame_total = stacked.shape[0]
    padded = jnp.pad(stacked, ((1, 1),) + ((0, 0),) * (stacked.ndim - 1))
    return jnp.concatenate([padded[offset:offset + frame_total] for offset in range(3)], axis=1)

def frame_attention(inputs):
    queries, key_rows, value_rows, visible = inputs
    head_size = D // HEADS
    query_heads = queries.reshape(queries.shape[0], HEADS, head_size)
    key_heads = key_rows.reshape(key_rows.shape[0], HEADS, head_size)
    value_heads = value_rows.reshape(value_rows.shape[0], HEADS, head_size)
    scores = jnp.einsum('qhd,khd->hqk', query_heads, key_heads, precision=highest) * SCALE
    scores = low_back(scores)
    scores = jnp.where(visible[None, None, :] > 0, scores, -1000000000.0)
    weights = low(jax.nn.softmax(scores, axis=-1))
    blended = jnp.einsum('hqk,khd->qhd', weights, value_heads, precision=highest)
    return blended.reshape(queries.shape[0], D)

def clip_forward(params, clip_tokens, visible):
    attn_gain, attn_shift, w_qkv, query_bias, value_bias, w_proj, proj_bias, mlp_gain, mlp_shift, w_expand, expand_bias, w_reduce, reduce_bias = params
    layout = (FRAMES, FRAME_CAP, D)
    flattened = clip_tokens.reshape(-1, D)
    normed = low(layer_norm(flattened, attn_gain, attn_shift))
    joined = jnp.dot(normed, w_qkv, precision=highest)
    queries = low(low_back(joined[:, :D] + query_bias))
    key_rows = low(low_back(joined[:, D:2 * D]))
    value_rows = low(low_back(joined[:, 2 * D:] + value_bias))
    key_windows = windows(key_rows.reshape(layout))
    value_windows = windows(value_rows.reshape(layout))
    mask_windows = windows(visible)
    blended = lax.map(jax.checkpoint(frame_attention), (queries.reshape(layout), key_windows, value_windows, mask_windows))
    blended = low(low_back(blended.reshape(-1, D)))
    branch = low_back(jnp.dot(blended, w_proj, precision=highest) + proj_bias)
    hidden = flattened + branch
    second = low(layer_norm(hidden, mlp_gain, mlp_shift))
    expanded = low_back(jnp.dot(second, w_expand, precision=highest) + expand_bias)
    activated = low(jax.nn.gelu(expanded, approximate=False))
    output = hidden + jnp.dot(activated, w_reduce, precision=highest) + reduce_bias
    return output.reshape(layout)

def reference(tokens, attn_gain, attn_shift, w_qkv, query_bias, value_bias, w_proj, proj_bias, mlp_gain, mlp_shift, w_expand, expand_bias, w_reduce, reduce_bias, cotangent, resolution, frame_count):
    params = tuple((weight.astype(jnp.float32) for weight in (attn_gain, attn_shift, w_qkv, query_bias, value_bias, w_proj, proj_bias, mlp_gain, mlp_shift, w_expand, expand_bias, w_reduce, reduce_bias)))

    def per_clip(totals, inputs):
        clip_tokens, clip_cotangent, clip_resolution, clip_frames = inputs
        visible = ((jnp.arange(FRAME_CAP)[None, :] < clip_resolution) & (jnp.arange(FRAMES)[:, None] < clip_frames)).astype(jnp.float32)
        output, pullback = jax.vjp(lambda weights, layer_input: clip_forward(weights, layer_input, visible), params, clip_tokens.astype(jnp.float32))
        gradients, grad_input = pullback(clip_cotangent.astype(jnp.float32) * visible[:, :, None])
        totals = jax.tree.map(jnp.add, totals, gradients)
        return (totals, (output.astype(jnp.bfloat16), grad_input))
    starting = jax.tree.map(jnp.zeros_like, params)
    totals, (activations, grad_tokens) = lax.scan(per_clip, starting, (tokens, cotangent, resolution, frame_count))
    squares = jnp.float32(0.0)
    for gradient in totals:
        squares = squares + jnp.sum(gradient * gradient)
    grad_norm = jnp.sqrt(squares)
    grad_attn_gain, grad_attn_shift, grad_w_qkv, grad_query_bias, grad_value_bias, grad_w_proj, grad_proj_bias, grad_mlp_gain, grad_mlp_shift, grad_w_expand, grad_expand_bias, grad_w_reduce, grad_reduce_bias = totals
    return (activations, grad_tokens, grad_attn_gain, grad_attn_shift, grad_w_qkv, grad_query_bias, grad_value_bias, grad_w_proj, grad_proj_bias, grad_mlp_gain, grad_mlp_shift, grad_w_expand, grad_expand_bias, grad_w_reduce, grad_reduce_bias, grad_norm)
```

```python
import functools
import jax
import jax.numpy as jnp
from jax import lax
from jax.sharding import PartitionSpec as P
from jax.experimental import pallas as pl
from jax.experimental.pallas import tpu as pltpu

T = 324
F = 336
D = 384
FF = 1536
N = 4
PAIRS = 3
EPS = 1e-6
NEG = -1e9
PAD = -1e30
LANES = 128
CHUNK = 512
f32 = jnp.float32
bf16 = jnp.bfloat16
NT = (((1,), (1,)), ((), ()))
NN = (((1,), (0,)), ((), ()))
TN = (((0,), (0,)), ((), ()))
MESH = pl.DeviceIdType.MESH


def dot(a, b, dims=NN):
    return lax.dot_general(a, b, dims, preferred_element_type=f32)


def rows_of(slot):
    return pl.ds(pl.multiple_of(slot * F, 16), F)


def live_rows_of(slot):
    return pl.ds(pl.multiple_of(slot * F, 16), T)


def normalise(x):
    centre = x - jnp.mean(x, axis=1, keepdims=True)
    spread = jnp.mean(centre * centre, axis=1, keepdims=True)
    inverse = lax.rsqrt(spread + EPS)
    return centre * inverse, inverse


def norm_back(grad, scaled, inverse, gain):
    e = grad * gain
    return inverse * (
        e - jnp.mean(e, axis=1, keepdims=True) - scaled * jnp.mean(e * scaled, axis=1, keepdims=True)
    )


def gelu_parts(x):
    u = jnp.exp(-0.5 * (x * x))
    t = 1.0 / (1.0 + 0.23164188844 * jnp.abs(x))
    p = t * (0.127414796 + t * (-0.142248368 + t * (0.7107068705 + t * (-0.7265760135 + t * 0.5307027145))))
    h = p * u
    cdf = jnp.where(x >= 0, 1.0 - h, h)
    return x * cdf, cdf + x * (u * 0.3989422804014327)


def column_sum(x):
    return jnp.sum(x, axis=0, keepdims=True)
EARLY = 10752
LATE = 3840


def main_kernel(
    tokens, cot, w_qkv, w_proj, w_expand, w_reduce, vec_d, vec_ff, res, cnt,
    act_out, grad_out, early_out, late_out,
    x, up0, wq, wp, we, wr, n, q, k, v, e0, e, bl, inv, hid, sec, up, a, ge, gh, gb, gbl, gj,
    hsend, hrecv, ostage, gstage, early, late, acc_d, acc_ff, lsem, osem, hsem,
):
    z = lax.axis_index("frame")
    other = 1 - z

    def place(s):
        return s + z * (3 - 2 * s)

    local = []

    def fetch(src, dst):
        c = pltpu.make_async_copy(src, dst, lsem.at[len(local)])
        c.start()
        local.append(c)
        return c

    cx = [fetch(tokens.at[0, place(s)], x.at[s]) for s in range(N)]
    cq = [
        fetch(w_qkv.at[:, pl.ds((t * PAIRS + p) * LANES, LANES)], wq.at[:, pl.ds((p * 3 + t) * LANES, LANES)])
        for p in range(PAIRS) for t in range(3)
    ]
    barrier = pltpu.get_barrier_semaphore()
    pl.semaphore_signal(barrier, inc=1, device_id={"frame": other}, device_id_type=MESH)
    cp = fetch(w_proj, wp)
    ce = fetch(w_expand, we)
    cr = fetch(w_reduce, wr)
    cc = [fetch(cot.at[0, place(s)], up0.at[s]) for s in range(N)]

    def vec(i):
        return vec_d[pl.ds(i, 1), :]

    attn_gain, attn_shift, query_bias, value_bias = vec(0), vec(1), vec(2), vec(3)
    proj_bias, mlp_gain, mlp_shift, reduce_bias = vec(4), vec(5), vec(6), vec(7)

    def limit(s):
        frame = s + z * (7 - 2 * s)
        return jnp.where(frame < cnt[0], res[0], 0)

    for ref in (n, sec, up, a, ge, gb):
        for s in range(N):
            ref[pl.ds(s * F + T, F - T), :] = jnp.zeros((F - T, ref.shape[1]), ref.dtype)
    for p in range(PAIRS):
        for s in range(N):
            gbl[p, pl.ds(s * F + T, F - T), :] = jnp.zeros((F - T, LANES), bf16)
    row = lax.broadcasted_iota(jnp.int32, (F, LANES), 0)
    lane = lax.broadcasted_iota(jnp.int32, (F, LANES), 1)
    low = lane < 64

    pl.semaphore_wait(barrier, 1)
    halo = pltpu.make_async_remote_copy(
        src_ref=tokens.at[0, place(N - 1)], dst_ref=x.at[N], send_sem=hsem.at[0], recv_sem=hsem.at[1],
        device_id={"frame": other}, device_id_type=MESH,
    )
    halo.start()

    def put_kv(s, p, keys, values):
        k[p, rows_of(s), :] = jnp.where(row < limit(s), keys, 0.0).astype(bf16)
        v[p, rows_of(s), pl.ds(0, LANES)] = jnp.where(
            row < T, values + value_bias[:, p * LANES:(p + 1) * LANES], 0.0
        ).astype(bf16)
        v[p, rows_of(s), pl.ds(LANES, LANES)] = jnp.ones((F, LANES), bf16)

    for c in cx + cq:
        c.wait()

    def project(s, carry):
        scaled, _ = normalise(x[s].astype(f32))
        n[live_rows_of(s), :] = (scaled * attn_gain + attn_shift).astype(bf16)
        joined = dot(n[rows_of(s), :], wq[...])
        for p in range(PAIRS):
            block = joined[:, p * D:(p + 1) * D]
            biased = (block[:, :LANES] + query_bias[:, p * LANES:(p + 1) * LANES]).astype(bf16)
            q[p, rows_of(s), :] = biased * jnp.asarray(0.125, bf16)
            put_kv(s, p, block[:, LANES:2 * LANES], block[:, 2 * LANES:])
        return carry

    lax.fori_loop(0, N, project, 0)

    halo.wait()
    scaled, _ = normalise(x[N].astype(f32))
    n[pl.ds(N * F, T), :] = (scaled * attn_gain + attn_shift).astype(bf16)
    n[pl.ds(N * F + T, F - T), :] = jnp.zeros((F - T, D), bf16)
    for p in range(PAIRS):
        block = dot(n[pl.ds(N * F, F), :], wq[:, pl.ds(p * D + LANES, 2 * LANES)])
        put_kv(N, p, block[:, :LANES], block[:, LANES:])

    def window(j):
        return list(range(max(j - 1, 0), j + 2))

    def span(j):
        w = window(j)
        return pl.ds(w[0] * F, len(w) * F)

    def bias_of(j):
        w = window(j)
        at = lax.broadcasted_iota(jnp.int32, (1, len(w) * F), 1)
        out = jnp.zeros((1, len(w) * F), f32)
        for i, s in enumerate(w):
            inside = (at >= i * F) & (at < (i + 1) * F)
            out = jnp.where(inside & (at >= i * F + limit(s)), NEG, out)
            out = jnp.where(inside & (at >= i * F + T), PAD, out)
        return out

    def half(value, h):
        zero = jnp.zeros_like(value)
        return jnp.where(low, value, zero) if h == 0 else jnp.where(low, zero, value)

    def weights_at(p, j, h):
        if j == 0:
            return e0.at[p, pl.ds(h * F, F)]
        return e.at[p * 3 + j - 1, pl.ds(h * F, F)]

    def forward(p, carry):
        order = [(j, h) for j in range(N) for h in range(2)]

        def scores(j, h):
            return dot(half(q[p, pl.ds(j * F, F), :], h), k[p, span(j), :], NT) + bias_of(j)

        s = scores(*order[0])
        held = []
        for i, (j, h) in enumerate(order):
            later = scores(*order[i + 1]) if i + 1 < len(order) else None
            largest = jnp.max(s, axis=1, keepdims=True)
            ex = jnp.exp(s - largest).astype(bf16)
            weights_at(p, j, h)[...] = ex
            o = dot(ex, v[p, span(j), :])
            total = o[:, LANES:]
            if j == 0:
                total = total + T * jnp.exp(NEG - largest)
            held.append((o[:, :LANES], 1.0 / total))
            if h == 1:
                (oa, ia), (ob, ib) = held
                held = []
                both = jnp.where(low, ia, ib)
                inv[p, pl.ds(j * F, F), :] = both
                bl[p, pl.ds(j * F, F), :] = (jnp.where(low, oa, ob) * both).astype(bf16)
            s = later
        return carry

    lax.fori_loop(0, PAIRS, forward, 0)

    for c in [cp, ce, cr] + cc:
        c.wait()
    acc_d[...] = jnp.zeros_like(acc_d)
    acc_ff[...] = jnp.zeros_like(acc_ff)
    live_row = lax.broadcasted_iota(jnp.int32, (T, D), 0)

    def mlp(j, carry):
        blended = jnp.concatenate([bl[p, live_rows_of(j), :] for p in range(PAIRS)], axis=1)
        hidden = x[j].astype(f32) + dot(blended, wp[...]) + proj_bias
        scaled, inverse = normalise(hidden)
        second = (scaled * mlp_gain + mlp_shift).astype(bf16)
        sec[live_rows_of(j), :] = second
        upstream = jnp.where(live_row < limit(j), up0[j].astype(f32), 0.0)
        up_low = upstream.astype(bf16)
        up[live_rows_of(j), :] = up_low
        output = hidden + reduce_bias
        grad_second = jnp.zeros((T, D), f32)
        for c in range(FF // CHUNK):
            cols = pl.ds(c * CHUNK, CHUNK)
            expanded = dot(second, we[:, cols]) + vec_ff[:, cols]
            gelu, slope = gelu_parts(expanded)
            low_gelu = gelu.astype(bf16)
            a[live_rows_of(j), cols] = low_gelu
            output = output + dot(low_gelu, wr[cols, :])
            grad = dot(up_low, wr[cols, :], NT) * slope
            grad_low = grad.astype(bf16)
            ge[live_rows_of(j), cols] = grad_low
            acc_ff[:, cols] += column_sum(grad_low.astype(f32))
            grad_second = grad_second + dot(grad_low, we[:, cols], NT)
        ostage[j] = output.astype(bf16)
        pltpu.make_async_copy(ostage.at[j], act_out.at[0, place(j)], osem.at[j]).start()
        acc_d[pl.ds(0, 1), :] += column_sum(upstream)
        acc_d[pl.ds(1, 1), :] += column_sum(grad_second * scaled)
        acc_d[pl.ds(2, 1), :] += column_sum(grad_second)
        grad_hidden = upstream + norm_back(grad_second, scaled, inverse, mlp_gain)
        gh[j] = grad_hidden
        branch = grad_hidden.astype(bf16)
        gb[live_rows_of(j), :] = branch
        acc_d[pl.ds(3, 1), :] += column_sum(branch.astype(f32))
        grad_blended = dot(branch, wp[...], NT).astype(bf16)
        for p in range(PAIRS):
            gbl[p, live_rows_of(j), :] = grad_blended[:, p * LANES:(p + 1) * LANES]
        return carry

    lax.fori_loop(0, N, mlp, 0)

    def pack(ref, base, block):
        block = block.astype(bf16)
        for t in range(block.shape[1] // LANES):
            ref[pl.ds(base + t * D, D), :] = block[:, t * LANES:(t + 1) * LANES]

    def pack_vectors(ref, base, rows, vectors):
        pieces = [w[:, t * LANES:(t + 1) * LANES] for w in vectors for t in range(w.shape[1] // LANES)]
        pieces.append(jnp.zeros((rows - len(pieces), LANES), f32))
        ref[pl.ds(base, rows), :] = jnp.concatenate(pieces, axis=0).astype(bf16)

    def big_weights(c, carry):
        cols = pl.ds(pl.multiple_of(c * D, LANES), D)
        base = pl.multiple_of(c * 3 * D, 16)
        pack(early, base, dot(sec[...], ge[:, cols], TN))
        pack(early, base + 12 * D, dot(up[...], a[:, cols], TN))
        return carry

    lax.fori_loop(0, FF // D, big_weights, 0)
    blended = jnp.concatenate([bl[p] for p in range(PAIRS)], axis=1)
    pack(early, 24 * D, dot(blended, gb[...], TN))
    pack_vectors(
        early, 27 * D, EARLY - 27 * D,
        [acc_d[pl.ds(0, 1), :], acc_ff[...], acc_d[pl.ds(1, 1), :], acc_d[pl.ds(2, 1), :], acc_d[pl.ds(3, 1), :]],
    )
    ce_out = pltpu.make_async_copy(early, early_out, osem.at[8])
    ce_out.start()

    def backward(p, carry):
        order = [(j, h) for j in (3, 2, 1, 0) for h in range(2)]
        prepared = {}

        def prepare(j):
            at = pl.ds(j * F, F)
            g = (gbl[p, at, :].astype(f32) * inv[p, at, :]).astype(bf16)
            product = g.astype(f32) * (-bl[p, at, :].astype(f32))
            high = product.astype(bf16)
            rest = pltpu.roll(product - high.astype(f32), 64, 1).astype(bf16)
            return g, high, rest

        def grad_weights(j, h):
            if j not in prepared:
                prepared[j] = prepare(j)
            g, high, rest = prepared[j]
            extra = jnp.where(low, high, rest) if h == 0 else jnp.where(low, rest, high)
            return dot(jnp.concatenate([half(g, h), extra], axis=1), v[p, span(j), :], NT)

        sums = {}

        def add(s, part):
            sums[s] = part if s not in sums else [y + w for y, w in zip(sums[s], part)]

        dp = grad_weights(*order[0])
        scores = []
        queries = []
        sent = None
        for i, (j, h) in enumerate(order):
            later = grad_weights(*order[i + 1]) if i + 1 < len(order) else None
            ds = (dp * weights_at(p, j, h)[...].astype(f32)).astype(bf16)
            scores.append(ds)
            queries.append(dot(ds, k[p, span(j), :]))
            if h == 1:
                at = pl.ds(j * F, F)
                gj[p, at, pl.ds(0, LANES)] = (jnp.where(low, queries[0], queries[1]) * 0.125).astype(bf16)
                qq = q[p, at, :]
                g = prepared[j][0]
                dk = dot(
                    jnp.concatenate([half(qq, 0), half(qq, 1)], axis=0), jnp.concatenate(scores, axis=0), TN
                ).T
                both = e0[p] if j == 0 else e[p * 3 + j - 1]
                dv = dot(jnp.concatenate([half(g, 0), half(g, 1)], axis=0), both, TN).T
                for t, s in enumerate(window(j)):
                    add(s, [dk[t * F:(t + 1) * F], dv[t * F:(t + 1) * F]])
                scores, queries = [], []
                if j == 3:
                    hsend[p, 0] = sums[N][0].astype(bf16)
                    hsend[p, 1] = sums[N][1].astype(bf16)
                    sent = pltpu.make_async_remote_copy(
                        src_ref=hsend.at[p], dst_ref=hrecv.at[p], send_sem=hsem.at[2 + p], recv_sem=hsem.at[5 + p],
                        device_id={"frame": other}, device_id_type=MESH,
                    )
                    sent.start()
            dp = later
        for s in range(N - 1):
            for t in range(2):
                gj[p, pl.ds(s * F, F), pl.ds((1 + t) * LANES, LANES)] = sums[s][t].astype(bf16)
        sent.wait()
        for t in range(2):
            gj[p, pl.ds(3 * F, F), pl.ds((1 + t) * LANES, LANES)] = (
                sums[3][t] + hrecv[p, t].astype(f32)
            ).astype(bf16)
        pack(late, pl.multiple_of(p * 3 * D, 16), dot(n[pl.ds(0, N * F), :], gj[p], TN))
        return carry

    lax.fori_loop(0, PAIRS, backward, 0)

    acc_d[...] = jnp.zeros_like(acc_d)

    def finish(j, carry):
        grads = jnp.concatenate([gj[p, rows_of(j), :] for p in range(PAIRS)], axis=1)
        for p in range(PAIRS):
            acc_d[pl.ds(2, 1), p * LANES:(p + 1) * LANES] += column_sum(grads[:, p * D:p * D + LANES].astype(f32))
            acc_d[pl.ds(3, 1), p * LANES:(p + 1) * LANES] += column_sum(
                grads[:, p * D + 2 * LANES:(p + 1) * D].astype(f32)
            )
        grad_normed = dot(grads, wq[...], NT)[:T]
        scaled, inverse = normalise(x[j].astype(f32))
        acc_d[pl.ds(0, 1), :] += column_sum(grad_normed * scaled)
        acc_d[pl.ds(1, 1), :] += column_sum(grad_normed)
        gstage[j] = gh[j] + norm_back(grad_normed, scaled, inverse, attn_gain)
        pltpu.make_async_copy(gstage.at[j], grad_out.at[0, place(j)], osem.at[4 + j]).start()
        return carry

    lax.fori_loop(0, N, finish, 0)
    pack_vectors(
        late, 9 * D, LATE - 9 * D,
        [acc_d[pl.ds(2, 1), :], acc_d[pl.ds(3, 1), :], acc_d[pl.ds(0, 1), :], acc_d[pl.ds(1, 1), :]],
    )
    cl_out = pltpu.make_async_copy(late, late_out, osem.at[9])
    cl_out.start()
    for j in range(N):
        pltpu.make_async_copy(ostage.at[j], act_out.at[0, place(j)], osem.at[j]).wait()
        pltpu.make_async_copy(gstage.at[j], grad_out.at[0, place(j)], osem.at[4 + j]).wait()
    ce_out.wait()
    cl_out.wait()


def run_main(tokens, cot, w_qkv, w_proj, w_expand, w_reduce, vec_d, vec_ff, res, cnt):
    hbm = pl.BlockSpec(memory_space=pl.ANY)
    vmem = pl.BlockSpec(memory_space=pltpu.VMEM)
    smem = pl.BlockSpec(memory_space=pltpu.SMEM)
    R = N * F
    V = pltpu.VMEM
    scratch = [
        V((N + 1, T, D), bf16), V((N, T, D), bf16), V((D, 3 * D), bf16), V((D, D), bf16), V((D, FF), bf16), V((FF, D), bf16),
        V((R + F, D), bf16), V((PAIRS, R, LANES), bf16), V((PAIRS, R + F, LANES), bf16), V((PAIRS, R + F, 2 * LANES), bf16),
        V((PAIRS, 2 * F, 2 * F), bf16), V((PAIRS * 3, 2 * F, 3 * F), bf16),
        V((PAIRS, R, LANES), bf16), V((PAIRS, R, LANES), f32), V((8, 128), f32),
        V((R, D), bf16), V((R, D), bf16), V((R, FF), bf16), V((R, FF), bf16), V((N, T, D), f32), V((R, D), bf16),
        V((PAIRS, R, LANES), bf16), V((PAIRS, R, D), bf16),
        V((PAIRS, 2, F, LANES), bf16), V((PAIRS, 2, F, LANES), bf16), V((N, T, D), bf16), V((N, T, D), f32),
        V((EARLY, LANES), bf16), V((LATE, LANES), bf16), V((8, D), f32), V((1, FF), f32),
        pltpu.SemaphoreType.DMA((24,)), pltpu.SemaphoreType.DMA((10,)), pltpu.SemaphoreType.DMA((8,)),
    ]
    return pl.pallas_call(
        main_kernel,
        out_shape=[
            jax.ShapeDtypeStruct((1, N, T, D), bf16), jax.ShapeDtypeStruct((1, N, T, D), f32),
            jax.ShapeDtypeStruct((EARLY, LANES), bf16), jax.ShapeDtypeStruct((LATE, LANES), bf16),
        ],
        in_specs=[hbm] * 6 + [vmem] * 2 + [smem] * 2,
        out_specs=[hbm] * 4,
        scratch_shapes=scratch,
        compiler_params=pltpu.CompilerParams(
            collective_id=0, has_side_effects=True, vmem_limit_bytes=63 * 2**20
        ),
    )(tokens, cot, w_qkv, w_proj, w_expand, w_reduce, vec_d, vec_ff, res, cnt)


def unpack(early, late):
    e = early.astype(f32)
    w = late.astype(f32)

    def block(rows, base):
        return jnp.concatenate([rows[base + t * D:base + (t + 1) * D] for t in range(3)], axis=1)

    g_we = jnp.concatenate([block(e, c * 3 * D) for c in range(4)], axis=1)
    g_wr = jnp.concatenate([block(e, (c + 4) * 3 * D).T for c in range(4)], axis=0)
    g_wp = block(e, 24 * D)
    tail = e[27 * D:27 * D + 24].reshape(-1)
    g_rb, g_eb, g_mg, g_ms, g_pb = tail[:384], tail[384:1920], tail[1920:2304], tail[2304:2688], tail[2688:3072]
    g_wq = jnp.concatenate(
        [w[(p * 3 + t) * D:(p * 3 + t + 1) * D] for t in range(3) for p in range(PAIRS)], axis=1
    )
    tail = w[9 * D:9 * D + 12].reshape(-1)
    g_qb, g_vb, g_ag, g_as = tail[:384], tail[384:768], tail[768:1152], tail[1152:1536]
    return (g_ag, g_as, g_wq, g_qb, g_vb, g_wp, g_pb, g_mg, g_ms, g_we, g_eb, g_wr, g_rb)


def body(
    tokens, attn_gain, attn_shift, w_qkv, query_bias, value_bias, w_proj, proj_bias, mlp_gain, mlp_shift,
    w_expand, expand_bias, w_reduce, reduce_bias, cotangent, resolution, frame_count,
):
    vec_d = jnp.stack(
        [y.astype(f32) for y in (attn_gain, attn_shift, query_bias, value_bias, proj_bias, mlp_gain, mlp_shift, reduce_bias)]
    )
    vec_ff = expand_bias.astype(f32).reshape(1, FF)
    act, grad, early, late = run_main(
        tokens, cotangent, w_qkv, w_proj, w_expand, w_reduce, vec_d, vec_ff, resolution, frame_count
    )
    early, late = lax.psum((early, late), ("clip", "frame"))
    grads = unpack(early, late)
    squares = sum(jnp.sum(g * g) for g in grads)
    return (act, grad) + grads + (jnp.sqrt(squares),)


def solution(mesh):
    data = P("clip", "frame", None, None)
    return jax.shard_map(
        body,
        mesh=mesh,
        in_specs=(data,) + (P(),) * 13 + (data, P("clip"), P("clip")),
        out_specs=(data, data) + (P(),) * 14,
        check_vma=False,
    )
```

```python
import functools
import jax
import jax.numpy as jnp
from jax import lax
from jax.sharding import PartitionSpec as P
from jax.experimental import pallas as pl
from jax.experimental.pallas import tpu as pltpu

T = 324
F = 336
D = 384
FF = 1536
N = 4
PAIRS = 3
EPS = 1e-6
NEG = -1e9
PAD = -1e30
LANES = 128
CHUNK = 512
R = N * F
f32 = jnp.float32
bf16 = jnp.bfloat16
NT = (((1,), (1,)), ((), ()))
NN = (((1,), (0,)), ((), ()))
TN = (((0,), (0,)), ((), ()))
MESH = pl.DeviceIdType.MESH


def dot(a, b, dims=NN):
    return lax.dot_general(a, b, dims, preferred_element_type=f32)


def rows_of(slot):
    return pl.ds(pl.multiple_of(slot * F, 16), F)


def live_rows_of(slot):
    return pl.ds(pl.multiple_of(slot * F, 16), T)


def normalise(x):
    centre = x - jnp.mean(x, axis=1, keepdims=True)
    spread = jnp.mean(centre * centre, axis=1, keepdims=True)
    inverse = lax.rsqrt(spread + EPS)
    return centre * inverse, inverse


def norm_back(grad, scaled, inverse, gain):
    e = grad * gain
    return inverse * (
        e - jnp.mean(e, axis=1, keepdims=True) - scaled * jnp.mean(e * scaled, axis=1, keepdims=True)
    )


def gelu_parts(x):
    u = jnp.exp(-0.5 * (x * x))
    t = 1.0 / (1.0 + 0.23164188844 * jnp.abs(x))
    p = t * (0.127414796 + t * (-0.142248368 + t * (0.7107068705 + t * (-0.7265760135 + t * 0.5307027145))))
    h = p * u
    cdf = jnp.where(x >= 0, 1.0 - h, h)
    return x * cdf, cdf + x * (u * 0.3989422804014327)


def column_sum(x):
    return jnp.sum(x, axis=0, keepdims=True)


def coordinates():
    clip = lax.axis_index("clip")
    z_hi = lax.axis_index("frame")
    core = clip % 2
    x = (clip // 2) % 4
    z_lo = (clip // 8) % 2
    y = clip // 16
    return x, y, 2 * z_hi + z_lo, core


def device_at(x, y, z, core):
    return {"clip": ((y * 2 + z % 2) * 4 + x) * 2 + core, "frame": z // 2}


def along(axis, step):
    x, y, z, core = coordinates()
    if axis == 0:
        x = (x + step) % 4
    elif axis == 1:
        y = (y + step) % 4
    else:
        z = (z + step) % 4
    return device_at(x, y, z, core)


def across():
    x, y, z, core = coordinates()
    return device_at(x, y, z, 1 - core)


def enter():
    barrier = pltpu.get_barrier_semaphore()
    pl.semaphore_signal(barrier, inc=1, device_id=across(), device_id_type=MESH)
    for axis in range(3):
        for step in (1, 2, 3):
            pl.semaphore_signal(barrier, inc=1, device_id=along(axis, step), device_id_type=MESH)


def entered():
    pl.semaphore_wait(pltpu.get_barrier_semaphore(), 10)


def total_of(parts):
    out = parts[0].astype(f32)
    for part in parts[1:]:
        out = out + part.astype(f32)
    return out.astype(bf16)


class Sum:
    def __init__(self, rows, scatter, fin, src, rcore, r1, w1, r2, w2, r3, sems):
        self.rows, self.scatter = rows, scatter
        self.src, self.fin, self.rcore, self.r1, self.w1, self.r2, self.w2, self.r3, self.sems = (
            src, fin, rcore, r1, w1, r2, w2, r3, sems)
        self.core = coordinates()[3]
        self.half, self.part, self.chunk = rows // 2, rows // 6, rows // 24
        self.sub = rows // 96 if scatter else rows // 24
        self.open = []
        self.count = 0

    @staticmethod
    def scratch(rows, scatter):
        sub = rows // 96 if scatter else rows // 24
        return [
            pltpu.VMEM((rows, LANES), bf16), pltpu.VMEM((rows // 2, LANES), bf16),
            pltpu.VMEM((3, 3, rows // 24, LANES), bf16), pltpu.VMEM((3, rows // 24, LANES), bf16),
            pltpu.VMEM((3, 3, sub, LANES) if scatter else (3, 4, sub, LANES), bf16), pltpu.VMEM((3, sub, LANES), bf16),
            pltpu.VMEM((3, 4, sub, LANES), bf16),
            pltpu.SemaphoreType.DMA((2, 2 + 9 * (5 if scatter else 4))),
        ]

    def send(self, src, dst, device):
        copy = pltpu.make_async_remote_copy(
            src_ref=src, dst_ref=dst, send_sem=self.sems.at[0, self.count], recv_sem=self.sems.at[1, self.count],
            device_id=device, device_id_type=MESH,
        )
        self.count += 1
        copy.start()
        self.open.append(copy)

    def arrive(self):
        for copy in self.open:
            copy.wait()
        self.open = []

    def spot(self, part, level):
        position = coordinates()[(part + level) % 3]
        return position

    def at(self, base, rows):
        return pl.ds(pl.multiple_of(base, 16), rows)

    def home(self, part, level):
        base = self.core * self.half + part * self.part
        if level >= 1:
            base = base + self.spot(part, 0) * self.chunk
        if level >= 2 and self.scatter:
            base = base + self.spot(part, 1) * self.sub
        return base

    def step0(self):
        away = (1 - self.core) * self.half
        self.send(self.src.at[self.at(away, self.half)], self.rcore, across())

    def step1(self):
        self.arrive()
        mine = self.at(self.core * self.half, self.half)
        self.src[mine, :] = total_of([self.src[mine, :], self.rcore[...]])
        for part in range(3):
            for step in (1, 2, 3):
                target = self.home(part, 0) + (self.spot(part, 0) + step) % 4 * self.chunk
                self.send(self.src.at[self.at(target, self.chunk)], self.r1.at[part, step - 1], along(part, step))

    def step2(self):
        self.arrive()
        for part in range(3):
            own = self.src[self.at(self.home(part, 1), self.chunk), :]
            total = total_of([own] + [self.r1[part, i] for i in range(3)])
            self.w1[part] = total
            if not self.scatter:
                self.r2[part, self.spot(part, 1)] = total
        for part in range(3):
            for step in (1, 2, 3):
                if self.scatter:
                    target = (self.spot(part, 1) + step) % 4 * self.sub
                    self.send(self.w1.at[part, self.at(target, self.sub)], self.r2.at[part, step - 1], along((part + 1) % 3, step))
                else:
                    self.send(self.w1.at[part], self.r2.at[part, self.spot(part, 1)], along((part + 1) % 3, step))

    def step3(self):
        self.arrive()
        for part in range(3):
            if self.scatter:
                own = self.w1[part, self.at(self.spot(part, 1) * self.sub, self.sub), :]
                total = total_of([own] + [self.r2[part, i] for i in range(3)])
            else:
                total = total_of([self.r2[part, i] for i in range(4)])
            self.w2[part] = total
            self.r3[part, self.spot(part, 2)] = total
        for part in range(3):
            for step in (1, 2, 3):
                self.send(self.w2.at[part], self.r3.at[part, self.spot(part, 2)], along((part + 2) % 3, step))

    def step4(self):
        self.arrive()
        for part in range(3):
            here = self.at(self.home(part, 2), self.sub)
            self.fin[here, :] = total_of([self.r3[part, i] for i in range(4)])
        if self.scatter:
            self.spread(1, 2, self.sub)
        else:
            self.spread(0, 1, self.chunk)

    def step5(self):
        self.arrive()
        if self.scatter:
            self.spread(0, 1, self.chunk)
        else:
            self.last()

    def step6(self):
        self.arrive()
        if self.scatter:
            self.last()

    def step7(self):
        self.arrive()

    def spread(self, axis, level, rows):
        for part in range(3):
            here = self.fin.at[self.at(self.home(part, level), rows)]
            for step in (1, 2, 3):
                self.send(here, here, along((part + axis) % 3, step))

    def last(self):
        here = self.fin.at[self.at(self.core * self.half, self.half)]
        self.send(here, here, across())


EARLY = 10752
LATES = ((0, 1), (2,))
LATE = tuple(-(-(len(g) * 9 * LANES + 16) // 384) * 384 for g in LATES)


def main_kernel(
    tokens, cot, w_qkv, w_proj, w_expand, w_reduce,
    v_ag, v_as, v_qb, v_vb, v_pb, v_mg, v_ms, v_rb, v_eb, res, cnt,
    act_out, grad_out, early_out, late0_out, late1_out,
    x, up0, wq, wp, we, wr, n, q, k, v, e0, e, bl, sec, up, a, ge, gh, gb, gbl, hrecv,
    acc_d, acc_ff, lsem, osem, hsem, *rest,
):
    z = lax.axis_index("frame")
    gj = a
    jobs = [Sum(EARLY, True, ge, *rest[:8]), Sum(LATE[0], False, *rest[8:17]), Sum(LATE[1], False, *rest[17:26])]
    early = jobs[0].src
    outs = [early_out, late0_out, late1_out]
    other = 1 - z

    def place(s):
        return s + z * (3 - 2 * s)

    local = []

    def fetch(src, dst):
        c = pltpu.make_async_copy(src, dst, lsem.at[len(local)])
        c.start()
        local.append(c)
        return c

    cx = [fetch(tokens.at[0, place(s)], x.at[s]) for s in range(N)]
    cq = [
        fetch(w_qkv.at[:, pl.ds((t * PAIRS + p) * LANES, LANES)], wq.at[:, pl.ds((p * 3 + t) * LANES, LANES)])
        for p in range(PAIRS) for t in range(3)
    ]
    enter()
    cp = fetch(w_proj, wp)
    ce = fetch(w_expand, we)
    cr = fetch(w_reduce, wr)
    cc = [fetch(cot.at[0, place(s)], up0.at[s]) for s in range(N)]

    attn_gain, attn_shift, query_bias, value_bias, proj_bias, mlp_gain, mlp_shift, reduce_bias, expand_bias = [
        ref[...].astype(f32).reshape(1, ref.shape[0])
        for ref in (v_ag, v_as, v_qb, v_vb, v_pb, v_mg, v_ms, v_rb, v_eb)
    ]

    def limit(s):
        frame = s + z * (7 - 2 * s)
        return jnp.where(frame < cnt[0], res[0], 0)

    for ref in (n, sec, up, a, gb, *[q.at[p] for p in range(PAIRS)]):
        for s in range(N):
            ref[pl.ds(s * F + T, F - T), :] = jnp.zeros((F - T, ref.shape[1]), ref.dtype)
    for p in range(PAIRS):
        for s in range(N):
            gbl[p, pl.ds(s * F + T, F - T), :] = jnp.zeros((F - T, LANES), bf16)
        for s in range(N + 1):
            k[p, pl.ds(s * F + T, F - T), :] = jnp.zeros((F - T, LANES), bf16)
            v[p, pl.ds(s * F + T, F - T), :] = jnp.zeros((F - T, LANES), bf16)
    for t in range(FF // LANES * N):
        ge[pl.ds(t * F + T, F - T), :] = jnp.zeros((F - T, LANES), bf16)
    row = lax.broadcasted_iota(jnp.int32, (F, LANES), 0)
    lane = lax.broadcasted_iota(jnp.int32, (F, LANES), 1)
    low = lane < 64

    entered()
    halo = pltpu.make_async_remote_copy(
        src_ref=tokens.at[0, place(N - 1)], dst_ref=x.at[N], send_sem=hsem.at[0], recv_sem=hsem.at[1],
        device_id={"frame": other}, device_id_type=MESH,
    )
    halo.start()

    def put_kv(s, p, keys, values):
        k[p, live_rows_of(s), :] = jnp.where(row[:T] < limit(s), keys, 0.0).astype(bf16)
        v[p, live_rows_of(s), :] = (values + value_bias[:, p * LANES:(p + 1) * LANES]).astype(bf16)

    for c in cx + cq:
        c.wait()

    def project(s, carry):
        scaled, _ = normalise(x[s].astype(f32))
        n[live_rows_of(s), :] = scaled.astype(bf16)
        joined = dot((scaled * attn_gain + attn_shift).astype(bf16), wq[...])
        for p in range(PAIRS):
            block = joined[:, p * D:(p + 1) * D]
            biased = (block[:, :LANES] + query_bias[:, p * LANES:(p + 1) * LANES]).astype(bf16)
            q[p, live_rows_of(s), :] = biased * jnp.asarray(0.125, bf16)
            put_kv(s, p, block[:, LANES:2 * LANES], block[:, 2 * LANES:])
        return carry

    lax.fori_loop(0, N, project, 0)

    halo.wait()
    scaled, _ = normalise(x[N].astype(f32))
    normed = (scaled * attn_gain + attn_shift).astype(bf16)
    for p in range(PAIRS):
        block = dot(normed, wq[:, pl.ds(p * D + LANES, 2 * LANES)])
        put_kv(N, p, block[:, :LANES], block[:, LANES:])

    def window(j):
        return list(range(max(j - 1, 0), j + 2))

    def span(j):
        w = window(j)
        return pl.ds(w[0] * F, len(w) * F)

    def bias_of(j):
        w = window(j)
        at = lax.broadcasted_iota(jnp.int32, (1, len(w) * F), 1)
        out = jnp.zeros((1, len(w) * F), f32)
        for i, s in enumerate(w):
            inside = (at >= i * F) & (at < (i + 1) * F)
            out = jnp.where(inside & (at >= i * F + limit(s)), NEG, out)
            out = jnp.where(inside & (at >= i * F + T), PAD, out)
        return out

    def half(value, h):
        zero = jnp.zeros_like(value)
        return jnp.where(low, value, zero) if h == 0 else jnp.where(low, zero, value)

    def values_at(p, j):
        return jnp.concatenate([v[p, span(j), :], jnp.ones((len(window(j)) * F, LANES), bf16)], axis=1)

    def weights_at(p, j, h):
        if j == 0:
            return e0.at[p, pl.ds(h * F, F)]
        return e.at[p * 3 + j - 1, pl.ds(h * F, F)]

    def forward(p, carry):
        order = [(j, h) for j in range(N) for h in range(2)]

        def scores(j, h):
            return dot(half(q[p, pl.ds(j * F, F), :], h), k[p, span(j), :], NT) + bias_of(j)

        s = scores(*order[0])
        held = []
        for i, (j, h) in enumerate(order):
            later = scores(*order[i + 1]) if i + 1 < len(order) else None
            largest = jnp.max(s, axis=1, keepdims=True)
            ex = jnp.exp(s - largest).astype(bf16)
            weights_at(p, j, h)[...] = ex
            o = dot(ex, values_at(p, j))
            total = o[:, LANES:]
            if j == 0:
                total = total + T * jnp.exp(NEG - largest)
            held.append((o[:, :LANES], 1.0 / total))
            if h == 1:
                (oa, ia), (ob, ib) = held
                held = []
                both = jnp.where(low, ia, ib)
                gh[j, :, pl.ds(pl.multiple_of(p * LANES, LANES), LANES)] = both[:T]
                bl[p, pl.ds(j * F, F), :] = jnp.where(low, oa, ob) * both
            s = later
        return carry

    lax.fori_loop(0, PAIRS, forward, 0)

    for c in [cp, ce, cr] + cc:
        c.wait()
    acc_d[...] = jnp.zeros_like(acc_d)
    acc_ff[...] = jnp.zeros_like(acc_ff)
    live_row = lax.broadcasted_iota(jnp.int32, (T, D), 0)

    def mlp(j, carry):
        blended = jnp.concatenate([bl[p, live_rows_of(j), :].astype(bf16) for p in range(PAIRS)], axis=1)
        hidden = x[j].astype(f32) + dot(blended, wp[...]) + proj_bias
        scaled, inverse = normalise(hidden)
        second = (scaled * mlp_gain + mlp_shift).astype(bf16)
        sec[live_rows_of(j), :] = second
        upstream = jnp.where(live_row < limit(j), up0[j].astype(f32), 0.0)
        up_low = upstream.astype(bf16)
        up[live_rows_of(j), :] = up_low
        output = hidden + reduce_bias
        grad_second = jnp.zeros((T, D), f32)
        for c in range(FF // CHUNK):
            cols = pl.ds(c * CHUNK, CHUNK)
            expanded = dot(second, we[:, cols]) + expand_bias[:, c * CHUNK:(c + 1) * CHUNK]
            gelu, slope = gelu_parts(expanded)
            low_gelu = gelu.astype(bf16)
            a[live_rows_of(j), cols] = low_gelu
            output = output + dot(low_gelu, wr[cols, :])
            grad = dot(up_low, wr[cols, :], NT) * slope
            grad_low = grad.astype(bf16)
            for t in range(CHUNK // LANES):
                at = pl.multiple_of((c * (CHUNK // LANES) + t) * R + j * F, 16)
                ge[pl.ds(at, T), :] = grad_low[:, t * LANES:(t + 1) * LANES]
            acc_ff[:, cols] += column_sum(grad_low.astype(f32))
            grad_second = grad_second + dot(grad_low, we[:, cols], NT)
        up0[j] = output.astype(bf16)
        pltpu.make_async_copy(up0.at[j], act_out.at[0, place(j)], osem.at[j]).start()
        acc_d[pl.ds(0, 1), :] += column_sum(upstream)
        acc_d[pl.ds(1, 1), :] += column_sum(grad_second * scaled)
        acc_d[pl.ds(2, 1), :] += column_sum(grad_second)
        grad_hidden = upstream + norm_back(grad_second, scaled, inverse, mlp_gain)
        branch = grad_hidden.astype(bf16)
        gb[live_rows_of(j), :] = branch
        acc_d[pl.ds(3, 1), :] += column_sum(branch.astype(f32))
        grad_blended = (dot(branch, wp[...], NT).astype(bf16).astype(f32) * gh[j]).astype(bf16)
        gh[j] = grad_hidden
        for p in range(PAIRS):
            gbl[p, live_rows_of(j), :] = grad_blended[:, p * LANES:(p + 1) * LANES]
        return carry

    lax.fori_loop(0, N, mlp, 0)

    def pack(ref, base, block):
        block = block.astype(bf16)
        for t in range(block.shape[1] // LANES):
            ref[pl.ds(base + t * D, D), :] = block[:, t * LANES:(t + 1) * LANES]

    def pack_vectors(ref, base, rows, vectors):
        pieces = [w[:, t * LANES:(t + 1) * LANES] for w in vectors for t in range(w.shape[1] // LANES)]
        pieces.append(jnp.zeros((rows - len(pieces), LANES), f32))
        ref[pl.ds(base, rows), :] = jnp.concatenate(pieces, axis=0).astype(bf16)

    def big_weights(c, carry):
        cols = pl.ds(pl.multiple_of(c * D, LANES), D)
        base = pl.multiple_of(c * 3 * D, 16)
        pack(early, base, dot(sec[...], jnp.concatenate([ge[pl.ds(pl.multiple_of((c * 3 + t) * R, 16), R), :] for t in range(3)], axis=1), TN))
        pack(early, base + 12 * D, dot(up[...], a[:, cols], TN))
        return carry

    lax.fori_loop(0, FF // D, big_weights, 0)
    blended = jnp.concatenate([bl[p].astype(bf16) for p in range(PAIRS)], axis=1)
    pack(early, 24 * D, dot(blended, gb[...], TN))
    pack_vectors(
        early, 27 * D, EARLY - 27 * D,
        [acc_d[pl.ds(0, 1), :], acc_ff[...], acc_d[pl.ds(1, 1), :], acc_d[pl.ds(2, 1), :], acc_d[pl.ds(3, 1), :]],
    )
    jobs[0].step0()

    def site(p, j):
        E = jobs[0]
        steps = {(0, 1): E.step1, (2, 3): E.step2}
        if (p, j) in steps:
            steps[(p, j)]()

    def backward(p):
        order = [(j, h) for j in (3, 2, 1, 0) for h in range(2)]
        prepared = {}

        def prepare(j):
            at = pl.ds(j * F, F)
            g = gbl[p, at, :]
            product = g.astype(f32) * (-bl[p, at, :])
            high = product.astype(bf16)
            rest = pltpu.roll(product - high.astype(f32), 64, 1).astype(bf16)
            return g, high, rest

        def grad_weights(j, h):
            if j not in prepared:
                prepared[j] = prepare(j)
            g, high, rest = prepared[j]
            extra = jnp.where(low, high, rest) if h == 0 else jnp.where(low, rest, high)
            return dot(jnp.concatenate([half(g, h), extra], axis=1), values_at(p, j), NT)

        sums = {}

        def add(s, part):
            sums[s] = part if s not in sums else [y + w for y, w in zip(sums[s], part)]

        dp = grad_weights(*order[0])
        scores = []
        queries = []
        sent = None
        for i, (j, h) in enumerate(order):
            later = grad_weights(*order[i + 1]) if i + 1 < len(order) else None
            ds = (dp * weights_at(p, j, h)[...].astype(f32)).astype(bf16)
            scores.append(ds)
            queries.append(dot(ds, k[p, span(j), :]))
            if h == 1:
                at = pl.ds(j * F, F)
                gj[at, pl.ds(p * D, LANES)] = (jnp.where(low, queries[0], queries[1]) * 0.125).astype(bf16)
                qq = q[p, at, :]
                g = prepared[j][0]
                dk = dot(
                    jnp.concatenate([half(qq, 0), half(qq, 1)], axis=0), jnp.concatenate(scores, axis=0), TN
                ).T
                both = e0[p] if j == 0 else e[p * 3 + j - 1]
                dv = dot(jnp.concatenate([half(g, 0), half(g, 1)], axis=0), both, TN).T
                for t, s in enumerate(window(j)):
                    add(s, [dk[t * F:(t + 1) * F], dv[t * F:(t + 1) * F]])
                scores, queries = [], []
                if j == 3:
                    sec[pl.ds(0, F), pl.ds(p * LANES, LANES)] = sums[N][0].astype(bf16)
                    sec[pl.ds(F, F), pl.ds(p * LANES, LANES)] = sums[N][1].astype(bf16)
                    sent = pltpu.make_async_remote_copy(
                        src_ref=sec.at[pl.ds(0, 2 * F), pl.ds(p * LANES, LANES)], dst_ref=hrecv.at[p], send_sem=hsem.at[2 + p], recv_sem=hsem.at[5 + p],
                        device_id={"frame": other}, device_id_type=MESH,
                    )
                    sent.start()
            dp = later
            if h == 1:
                site(p, j)
        for s in range(N - 1):
            for t in range(2):
                gj[pl.ds(s * F, F), pl.ds(p * D + (1 + t) * LANES, LANES)] = sums[s][t].astype(bf16)
        sent.wait()
        for t in range(2):
            gj[pl.ds(3 * F, F), pl.ds(p * D + (1 + t) * LANES, LANES)] = (
                sums[3][t] + hrecv[p, pl.ds(t * F, F), :].astype(f32)
            ).astype(bf16)
        group = 0 if p in LATES[0] else 1
        at = LATES[group].index(p)
        columns = gj[:, pl.ds(p * D, D)]
        pack(jobs[1 + group].src, at * 3 * D, dot(n[...], columns, TN))
        columns_sum[p] = column_sum(columns.astype(f32))
        if at == len(LATES[group]) - 1:
            base = len(LATES[group]) * 3 * D
            pack_vectors(jobs[1 + group].src, base, LATE[group] - base, [columns_sum[i] for i in LATES[group]])
            jobs[1 + group].step0()

    columns_sum = {}
    for p in range(PAIRS):
        backward(p)

    def tail(finish):
        E, A, B = jobs
        E.step3(); A.step1()
        finish(0, 0)
        B.step1()
        finish(1, 0)
        E.step4(); A.step2()
        finish(2, 0)
        B.step2()
        finish(3, 0)
        A.step3()
        E.step5()
        B.step3()
        A.step4()
        B.step4()
        E.step6()
        A.step5()
        B.step5()
        A.step6(); B.step6(); E.step7()

    def finish(j, carry):
        grad_normed = dot(gj[live_rows_of(j), pl.ds(0, 3 * D)], wq[...], NT)
        scaled, inverse = normalise(x[j].astype(f32))
        gh[j] = gh[j] + norm_back(grad_normed, scaled, inverse, attn_gain)
        pltpu.make_async_copy(gh.at[j], grad_out.at[0, :, place(j), :], osem.at[4 + j]).start()
        return carry

    tail(finish)
    for i, job in enumerate(jobs):
        copy = pltpu.make_async_copy(job.fin.at[pl.ds(0, job.rows)], outs[i], osem.at[8 + i])
        copy.start()
    for j in range(N):
        pltpu.make_async_copy(up0.at[j], act_out.at[0, place(j)], osem.at[j]).wait()
        pltpu.make_async_copy(gh.at[j], grad_out.at[0, :, place(j), :], osem.at[4 + j]).wait()
    for i, job in enumerate(jobs):
        pltpu.make_async_copy(job.fin.at[pl.ds(0, job.rows)], outs[i], osem.at[8 + i]).wait()


def run_main(tokens, cot, w_qkv, w_proj, w_expand, w_reduce, *rest):
    hbm = pl.BlockSpec(memory_space=pl.ANY)
    vmem = pl.BlockSpec(memory_space=pltpu.VMEM)
    smem = pl.BlockSpec(memory_space=pltpu.SMEM)
    V = pltpu.VMEM
    scratch = [
        V((N + 1, T, D), bf16), V((N, T, D), bf16), V((D, 3 * D), bf16), V((D, D), bf16), V((D, FF), bf16), V((FF, D), bf16),
        V((R, D), bf16), V((PAIRS, R, LANES), bf16), V((PAIRS, R + F, LANES), bf16), V((PAIRS, R + F, LANES), bf16),
        V((PAIRS, 2 * F, 2 * F), bf16), V((PAIRS * 3, 2 * F, 3 * F), bf16),
        V((PAIRS, R, LANES), f32),
        V((R, D), bf16), V((R, D), bf16), V((R, FF), bf16), V((FF // LANES * R, LANES), bf16), V((N, T, D), f32), V((R, D), bf16),
        V((PAIRS, R, LANES), bf16),
        V((PAIRS, 2 * F, LANES), bf16), V((8, D), f32), V((1, FF), f32),
        pltpu.SemaphoreType.DMA((24,)), pltpu.SemaphoreType.DMA((11,)), pltpu.SemaphoreType.DMA((8,)),
    ] + Sum.scratch(EARLY, True) + [
        y for rows in LATE for y in [V((rows, LANES), bf16)] + Sum.scratch(rows, False)
    ]
    return pl.pallas_call(
        main_kernel,
        out_shape=[
            jax.ShapeDtypeStruct((1, N, T, D), bf16), jax.ShapeDtypeStruct((1, T, N, D), f32),
            jax.ShapeDtypeStruct((EARLY, LANES), bf16), jax.ShapeDtypeStruct((LATE[0], LANES), bf16),
            jax.ShapeDtypeStruct((LATE[1], LANES), bf16),
        ],
        in_specs=[hbm] * 6 + [vmem] * 9 + [smem] * 2,
        out_specs=[hbm] * 5,
        scratch_shapes=scratch,
        compiler_params=pltpu.CompilerParams(
            collective_id=0, has_side_effects=True, vmem_limit_bytes=66_900_000
        ),
    )(tokens, cot, w_qkv, w_proj, w_expand, w_reduce, *rest)


def final_kernel(
    early_in, late0_in, late1_in, wq_in, gain_ref, shift_ref,
    o_ag, o_as, o_wq, o_qb, o_vb, o_wp, o_pb, o_mg, o_ms, o_we, o_eb, o_wr, o_rb, o_norm,
    early, late0, late1, wq, s_wq, s_wp, s_we, s_wr, isem, osem,
):
    half = 12 * D
    pieces = [
        (early_in.at[pl.ds(half, half)], early.at[pl.ds(half, half)]), (early_in.at[pl.ds(0, half)], early.at[pl.ds(0, half)]),
        (early_in.at[pl.ds(2 * half, EARLY - 2 * half)], early.at[pl.ds(2 * half, EARLY - 2 * half)]),
        (late0_in, late0), (late1_in, late1), (wq_in, wq),
    ]
    fetches = [pltpu.make_async_copy(src, dst, isem.at[i]) for i, (src, dst) in enumerate(pieces)]
    for copy in fetches:
        copy.start()

    def square(total, block):
        return total + jnp.sum(block * block, axis=0, keepdims=True)

    total = jnp.zeros((1, LANES), f32)
    stores = []

    def store(src, dst):
        copy = pltpu.make_async_copy(src, dst, osem.at[len(stores)])
        copy.start()
        stores.append(copy)

    fetches[0].wait()
    for c in range(12):
        block = early[pl.ds(half + c * D, D), :].astype(f32)
        s_wr[pl.ds(c * LANES, LANES), :] = block.T
        total = square(total, block)
    store(s_wr, o_wr)
    fetches[1].wait()
    for c in range(12):
        block = early[pl.ds(c * D, D), :].astype(f32)
        s_we[:, pl.ds(c * LANES, LANES)] = block
        total = square(total, block)
    store(s_we, o_we)
    fetches[2].wait()
    for c in range(3):
        block = early[pl.ds(2 * half + c * D, D), :].astype(f32)
        s_wp[:, pl.ds(c * LANES, LANES)] = block
        total = square(total, block)
    store(s_wp, o_wp)
    tail = early[pl.ds(27 * D, 32), :].astype(f32)
    total = square(total, tail[:24])
    lines = [tail[i:i + 1] for i in range(24)]

    def line(parts):
        return jnp.concatenate(parts, axis=1).reshape(len(parts) * LANES)

    o_rb[...] = line(lines[:3])
    o_eb[...] = line(lines[3:15])
    o_mg[...] = line(lines[15:18])
    o_ms[...] = line(lines[18:21])
    o_pb[...] = line(lines[21:24])

    def column(ref):
        row = ref[...].reshape(1, D)
        return jnp.broadcast_to(row, (LANES, D)).T

    gain, shift = column(gain_ref), column(shift_ref)
    for copy in fetches[3:]:
        copy.wait()
    along_gain = jnp.zeros((D, LANES), f32)
    along_shift = jnp.zeros((D, LANES), f32)
    sums = {}
    for group, ref in ((0, late0), (1, late1)):
        pairs = LATES[group]
        extra = ref[pl.ds(len(pairs) * 3 * D, 16), :].astype(f32)
        for i, p in enumerate(pairs):
            for t in range(3):
                moment = ref[pl.ds((i * 3 + t) * D, D), :].astype(f32)
                summed = extra[i * 3 + t:i * 3 + t + 1]
                sums[t, p] = summed
                cols = pl.ds((t * PAIRS + p) * LANES, LANES)
                weight = wq[:, cols].astype(f32)
                block = gain * moment + shift * summed
                s_wq[:, cols] = block
                total = square(total, block)
                along_gain = along_gain + weight * moment
                along_shift = along_shift + weight * summed
    store(s_wq, o_wq)
    grad_gain = jnp.sum(along_gain.T, axis=0, keepdims=True)
    grad_shift = jnp.sum(along_shift.T, axis=0, keepdims=True)
    o_ag[...] = grad_gain.reshape(D)
    o_as[...] = grad_shift.reshape(D)
    o_qb[...] = line([sums[0, p] for p in range(PAIRS)])
    o_vb[...] = line([sums[2, p] for p in range(PAIRS)])
    for p in range(PAIRS):
        total = square(square(total, sums[0, p]), sums[2, p])
        cols = slice(p * LANES, (p + 1) * LANES)
        total = square(square(total, grad_gain[:, cols]), grad_shift[:, cols])
    o_norm[...] = jnp.sqrt(jnp.sum(total, axis=1, keepdims=True))
    for copy in stores:
        copy.wait()


def run_final(early, late0, late1, w_qkv, gain, shift):
    hbm = pl.BlockSpec(memory_space=pl.ANY)
    vmem = pl.BlockSpec(memory_space=pltpu.VMEM)
    V = pltpu.VMEM
    vector = jax.ShapeDtypeStruct((D,), f32)

    def matrix(a, b):
        return jax.ShapeDtypeStruct((a, b), f32)

    shapes = [
        vector, vector, matrix(D, 3 * D), vector, vector, matrix(D, D), vector, vector, vector, matrix(D, FF),
        jax.ShapeDtypeStruct((FF,), f32), matrix(FF, D), vector, matrix(1, 1),
    ]
    return pl.pallas_call(
        final_kernel,
        out_shape=shapes,
        in_specs=[hbm] * 4 + [vmem] * 2,
        out_specs=[hbm if len(s.shape) == 2 and s.shape[0] > 1 else vmem for s in shapes],
        scratch_shapes=[
            V((EARLY, LANES), bf16), V((LATE[0], LANES), bf16), V((LATE[1], LANES), bf16), V((D, 3 * D), bf16),
            V((D, 3 * D), f32), V((D, D), f32), V((D, FF), f32), V((FF, D), f32),
            pltpu.SemaphoreType.DMA((6,)), pltpu.SemaphoreType.DMA((4,)),
        ],
        compiler_params=pltpu.CompilerParams(vmem_limit_bytes=40 * 2**20),
    )(early, late0, late1, w_qkv, gain, shift)


def body(
    tokens, attn_gain, attn_shift, w_qkv, query_bias, value_bias, w_proj, proj_bias, mlp_gain, mlp_shift,
    w_expand, expand_bias, w_reduce, reduce_bias, cotangent, resolution, frame_count,
):
    act, grad, early, late0, late1 = run_main(
        tokens, cotangent, w_qkv, w_proj, w_expand, w_reduce, attn_gain, attn_shift, query_bias, value_bias,
        proj_bias, mlp_gain, mlp_shift, reduce_bias, expand_bias, resolution, frame_count,
    )
    *grads, norm = run_final(early, late0, late1, w_qkv, attn_gain, attn_shift)
    return (act, jnp.transpose(grad, (0, 2, 1, 3)), *grads, norm.reshape(()))


def solution(mesh):
    data = P("clip", "frame", None, None)
    return jax.shard_map(
        body,
        mesh=mesh,
        in_specs=(data,) + (P(),) * 13 + (data, P("clip"), P("clip")),
        out_specs=(data, data) + (P(),) * 14,
        check_vma=False,
    )
```

```python
import functools
import jax
import jax.numpy as jnp
from jax import lax
from jax.sharding import PartitionSpec as P
from jax.experimental import pallas as pl
from jax.experimental.pallas import tpu as pltpu

T = 324
F = 336
D = 384
FF = 1536
N = 4
PAIRS = 3
EPS = 1e-6
NEG = -1e9
PAD = -1e30
LANES = 128
CHUNK = 256
MLP_FRAMES = 2
R = N * F
f32 = jnp.float32
bf16 = jnp.bfloat16
NT = (((1,), (1,)), ((), ()))
NN = (((1,), (0,)), ((), ()))
TN = (((0,), (0,)), ((), ()))
MESH = pl.DeviceIdType.MESH


def dot(a, b, dims=NN):
    return lax.dot_general(a, b, dims, preferred_element_type=f32)


def rows_of(slot):
    return pl.ds(pl.multiple_of(slot * F, 16), F)


def live_rows_of(slot):
    return pl.ds(pl.multiple_of(slot * F, 16), T)


def normalise(x):
    centre = x - jnp.mean(x, axis=1, keepdims=True)
    spread = jnp.mean(centre * centre, axis=1, keepdims=True)
    inverse = lax.rsqrt(spread + EPS)
    return centre * inverse, inverse


def norm_back(grad, scaled, inverse, gain):
    e = grad * gain
    return inverse * (
        e - jnp.mean(e, axis=1, keepdims=True) - scaled * jnp.mean(e * scaled, axis=1, keepdims=True)
    )


def gelu_parts(x):
    u = jnp.exp(-0.5 * (x * x))
    t = 1.0 / (1.0 + 0.23164188844 * jnp.abs(x))
    p = t * (0.127414796 + t * (-0.142248368 + t * (0.7107068705 + t * (-0.7265760135 + t * 0.5307027145))))
    h = p * u
    cdf = jnp.where(x >= 0, 1.0 - h, h)
    return x * cdf, cdf + x * (u * 0.3989422804014327)


def column_sum(x):
    return jnp.sum(x, axis=0, keepdims=True)


def coordinates():
    clip = lax.axis_index("clip")
    z_hi = lax.axis_index("frame")
    core = clip % 2
    x = (clip // 2) % 4
    z_lo = (clip // 8) % 2
    y = clip // 16
    return x, y, 2 * z_hi + z_lo, core


def device_at(x, y, z, core):
    return {"clip": ((y * 2 + z % 2) * 4 + x) * 2 + core, "frame": z // 2}


def along(axis, step):
    x, y, z, core = coordinates()
    if axis == 0:
        x = (x + step) % 4
    elif axis == 1:
        y = (y + step) % 4
    else:
        z = (z + step) % 4
    return device_at(x, y, z, core)


def across():
    x, y, z, core = coordinates()
    return device_at(x, y, z, 1 - core)


def enter():
    barrier = pltpu.get_barrier_semaphore()
    pl.semaphore_signal(barrier, inc=1, device_id=across(), device_id_type=MESH)
    for axis in range(3):
        for step in (1, 2, 3):
            pl.semaphore_signal(barrier, inc=1, device_id=along(axis, step), device_id_type=MESH)


def entered():
    pl.semaphore_wait(pltpu.get_barrier_semaphore(), 10)


def total_of(parts):
    out = parts[0].astype(f32)
    for part in parts[1:]:
        out = out + part.astype(f32)
    return out.astype(bf16)


def strip(base, rows):
    return pl.ds(pl.multiple_of(base, 16), rows)


class Sum:
    def __init__(self, rows, scatter, fin, offset, src, rcore, r1, w1, r2, w2, r3, sems):
        self.rows, self.scatter, self.offset = rows, scatter, offset
        self.src, self.fin, self.rcore, self.r1, self.w1, self.r2, self.w2, self.r3, self.sems = (
            src, fin, rcore, r1, w1, r2, w2, r3, sems)
        self.half, self.part, self.chunk = rows // 2, rows // 6, rows // 24
        self.sub = rows // 96 if scatter else rows // 24

    @staticmethod
    def scratch(rows, scatter):
        sub = rows // 96 if scatter else rows // 24
        return [
            pltpu.VMEM((rows, LANES), bf16), pltpu.VMEM((rows // 2, LANES), bf16),
            pltpu.VMEM((3, 3, rows // 24, LANES), bf16), pltpu.VMEM((3, rows // 24, LANES), bf16),
            pltpu.VMEM((3, 3, sub, LANES) if scatter else (3, 4, sub, LANES), bf16), pltpu.VMEM((3, sub, LANES), bf16),
            pltpu.VMEM((3, 4, sub, LANES), bf16),
            pltpu.SemaphoreType.DMA((2, 2 + 9 * (5 if scatter else 4))),
        ]

    def spot(self, part, level):
        return coordinates()[(part + level) % 3]

    def home(self, part, level):
        base = coordinates()[3] * self.half + part * self.part
        if level >= 1:
            base = base + self.spot(part, 0) * self.chunk
        if level >= 2 and self.scatter:
            base = base + self.spot(part, 1) * self.sub
        return base

    def copies(self, stage):
        core = coordinates()[3]
        out = []
        last = 6 if self.scatter else 5
        if stage == 0:
            out.append((self.src.at[strip((1 - core) * self.half, self.half)], self.rcore, across()))
        elif stage == last:
            here = self.fin.at[strip(self.offset + core * self.half, self.half)]
            out.append((here, here, across()))
        else:
            for part in range(3):
                for step in (1, 2, 3):
                    if stage == 1:
                        target = self.home(part, 0) + (self.spot(part, 0) + step) % 4 * self.chunk
                        out.append((self.src.at[strip(target, self.chunk)], self.r1.at[part, step - 1], along(part, step)))
                    elif stage == 2 and self.scatter:
                        target = (self.spot(part, 1) + step) % 4 * self.sub
                        out.append((self.w1.at[part, strip(target, self.sub)], self.r2.at[part, step - 1], along((part + 1) % 3, step)))
                    elif stage == 2:
                        out.append((self.w1.at[part], self.r2.at[part, self.spot(part, 1)], along((part + 1) % 3, step)))
                    elif stage == 3:
                        out.append((self.w2.at[part], self.r3.at[part, self.spot(part, 2)], along((part + 2) % 3, step)))
                    else:
                        axis, level, rows = (1, 2, self.sub) if self.scatter and stage == 4 else (0, 1, self.chunk)
                        here = self.fin.at[strip(self.offset + self.home(part, level), rows)]
                        out.append((here, here, along((part + axis) % 3, step)))
        first = 0 if stage == 0 else 1 + 9 * (stage - 1)
        return [
            pltpu.make_async_remote_copy(
                src_ref=src, dst_ref=dst, send_sem=self.sems.at[0, first + i], recv_sem=self.sems.at[1, first + i],
                device_id=device, device_id_type=MESH,
            )
            for i, (src, dst, device) in enumerate(out)
        ]

    def start(self, stage):
        for copy in self.copies(stage):
            copy.start()

    def arrive(self, stage):
        for copy in self.copies(stage):
            copy.wait()

    def step(self, stage):
        last = 6 if self.scatter else 5
        if stage > last + 1:
            return
        if stage > 0:
            self.arrive(stage - 1)
        if stage == 1:
            mine = strip(coordinates()[3] * self.half, self.half)
            self.src[mine, :] = total_of([self.src[mine, :], self.rcore[...]])
        for part in range(3):
            if stage == 2:
                own = self.src[strip(self.home(part, 1), self.chunk), :]
                total = total_of([own] + [self.r1[part, i] for i in range(3)])
                self.w1[part] = total
                if not self.scatter:
                    self.r2[part, self.spot(part, 1)] = total
            elif stage == 3:
                if self.scatter:
                    own = self.w1[part, strip(self.spot(part, 1) * self.sub, self.sub), :]
                    total = total_of([own] + [self.r2[part, i] for i in range(3)])
                else:
                    total = total_of([self.r2[part, i] for i in range(4)])
                self.w2[part] = total
                self.r3[part, self.spot(part, 2)] = total
            elif stage == 4:
                here = strip(self.offset + self.home(part, 2), self.sub)
                self.fin[here, :] = total_of([self.r3[part, i] for i in range(4)])
        if stage <= last:
            self.start(stage)


EARLY = 10752
LATES = ((0, 1), (2,))
LATE = tuple(-(-(len(g) * 9 * LANES + 16) // 384) * 384 for g in LATES)


def main_kernel(
    tokens, cot, w_qkv, w_proj, w_expand, w_reduce,
    v_ag, v_as, v_qb, v_vb, v_pb, v_mg, v_ms, v_rb, v_eb, res, cnt,
    act_out, grad_out, early_out, late0_out, late1_out,
    x, up0, wq, wp, we, wr, n, nh, q, k, v, e0, e, bl, trio, a, ge, gh, gbl, hrecv, act_t,
    acc_d, acc_ff, lsem, osem, hsem, *rest,
):
    z = lax.axis_index("frame")
    sec, up, gb = trio.at[0], trio.at[1], trio.at[2]
    gj = trio
    jobs = [Sum(EARLY, True, ge, 0, *rest[:8]), Sum(LATE[0], False, ge, EARLY + PAIRS * 2 * F, *rest[8:16]), Sum(LATE[1], False, rest[16], 0, *rest[17:25])]
    early = jobs[0].src
    outs = [early_out, late0_out, late1_out]
    other = 1 - z

    def place(s):
        return s + z * (3 - 2 * s)

    local = []

    def fetch(src, dst):
        c = pltpu.make_async_copy(src, dst, lsem.at[len(local)])
        c.start()
        local.append(c)
        return c

    cx = [fetch(tokens.at[0, place(s)], x.at[s]) for s in range(N)]
    cq = [
        fetch(w_qkv.at[:, pl.ds((t * PAIRS + p) * LANES, LANES)], wq.at[:, pl.ds((p * 3 + t) * LANES, LANES)])
        for p in range(PAIRS) for t in range(3)
    ]
    enter()
    cp = fetch(w_proj, wp)
    ce = fetch(w_expand, we)
    cr = fetch(w_reduce, wr)
    cc = [fetch(cot.at[0, place(s)], up0.at[s]) for s in range(N)]

    attn_gain, attn_shift, query_bias, value_bias, proj_bias, mlp_gain, mlp_shift, reduce_bias, expand_bias = [
        ref[...].astype(f32).reshape(1, ref.shape[0])
        for ref in (v_ag, v_as, v_qb, v_vb, v_pb, v_mg, v_ms, v_rb, v_eb)
    ]

    def limit(s):
        frame = s + z * (7 - 2 * s)
        return jnp.where(frame < cnt[0], res[0], 0)

    for ref in (n, nh, sec, up, a, gb, *[q.at[p] for p in range(PAIRS)]):
        for s in range(ref.shape[0] // F):
            ref[pl.ds(s * F + T, F - T), :] = jnp.zeros((F - T, ref.shape[1]), ref.dtype)
    for p in range(PAIRS):
        for s in range(N):
            gbl[p, pl.ds(s * F + T, F - T), :] = jnp.zeros((F - T, LANES), bf16)
        for s in range(N + 1):
            k[p, pl.ds(s * F + T, F - T), :] = jnp.zeros((F - T, LANES), bf16)
            v[p, pl.ds(s * F + T, F - T), :] = jnp.zeros((F - T, LANES), bf16)
    for t in range(FF // LANES * N):
        ge[pl.ds(t * F + T, F - T), :] = jnp.zeros((F - T, LANES), bf16)
    row = lax.broadcasted_iota(jnp.int32, (F, LANES), 0)
    lane = lax.broadcasted_iota(jnp.int32, (F, LANES), 1)
    low = lane < 64

    def put_kv(s, p, keys, values):
        k[p, live_rows_of(s), :] = jnp.where(row[:T] < limit(s), keys, 0.0).astype(bf16)
        v[p, live_rows_of(s), :] = (values + value_bias[:, p * LANES:(p + 1) * LANES]).astype(bf16)

    for c in cx + cq:
        c.wait()

    def project(s, carry):
        scaled, _ = normalise(x[s].astype(f32))
        n[live_rows_of(s), :] = scaled.astype(bf16)
        joined = dot((scaled * attn_gain + attn_shift).astype(bf16), wq[...])
        for p in range(PAIRS):
            block = joined[:, p * D:(p + 1) * D]
            biased = (block[:, :LANES] + query_bias[:, p * LANES:(p + 1) * LANES]).astype(bf16)
            q[p, live_rows_of(s), :] = biased * jnp.asarray(0.125, bf16)
            put_kv(s, p, block[:, LANES:2 * LANES], block[:, 2 * LANES:])
        return carry

    lax.fori_loop(0, N, project, 0)

    entered()
    halo = pltpu.make_async_remote_copy(
        src_ref=tokens.at[0, place(N - 1)], dst_ref=x.at[N], send_sem=hsem.at[0], recv_sem=hsem.at[1],
        device_id={"frame": other}, device_id_type=MESH,
    )
    halo.start()

    def window(j):
        return list(range(max(j - 1, 0), j + 2))

    def span(j):
        w = window(j)
        return pl.ds(w[0] * F, len(w) * F)

    def bias_of(j):
        w = window(j)
        at = lax.broadcasted_iota(jnp.int32, (1, len(w) * F), 1)
        out = jnp.zeros((1, len(w) * F), f32)
        for i, s in enumerate(w):
            inside = (at >= i * F) & (at < (i + 1) * F)
            out = jnp.where(inside & (at >= i * F + limit(s)), NEG, out)
            out = jnp.where(inside & (at >= i * F + T), PAD, out)
        return out

    def half(value, h):
        zero = jnp.zeros_like(value)
        return jnp.where(low, value, zero) if h == 0 else jnp.where(low, zero, value)

    def values_at(p, j):
        return jnp.concatenate([v[p, span(j), :], jnp.ones((len(window(j)) * F, LANES), bf16)], axis=1)

    def weights_at(p, j, h):
        if j == 0:
            return e0.at[p, pl.ds(h * F, F)]
        return e.at[p * 3 + j - 1, pl.ds(h * F, F)]

    def forward(units):
        order = [(p, j, h) for p, j in units for h in range(2)]

        def scores(p, j, h):
            return dot(half(q[p, pl.ds(j * F, F), :], h), k[p, span(j), :], NT) + bias_of(j)

        s = scores(*order[0])
        held = []
        for i, (p, j, h) in enumerate(order):
            later = scores(*order[i + 1]) if i + 1 < len(order) else None
            largest = jnp.max(s, axis=1, keepdims=True)
            ex = jnp.exp(s - largest).astype(bf16)
            weights_at(p, j, h)[...] = ex
            o = dot(ex, values_at(p, j))
            total = o[:, LANES:]
            if j == 0:
                total = total + T * jnp.exp(NEG - largest)
            held.append((o[:, :LANES], 1.0 / total))
            if h == 1:
                (oa, ia), (ob, ib) = held
                held = []
                both = jnp.where(low, ia, ib)
                gh[j, :, pl.ds(pl.multiple_of(p * LANES, LANES), LANES)] = both[:T]
                bl[p, pl.ds(j * F, F), :] = (jnp.where(low, oa, ob) * both).astype(bf16)
            s = later

    def inner(p, carry):
        forward([(p, j) for j in range(N - 1)])
        return carry

    lax.fori_loop(0, PAIRS, inner, 0)
    halo.wait()
    scaled, _ = normalise(x[N].astype(f32))
    nh[pl.ds(0, T), :] = scaled.astype(bf16)
    normed = (scaled * attn_gain + attn_shift).astype(bf16)
    for p in range(PAIRS):
        block = dot(normed, wq[:, pl.ds(p * D + LANES, 2 * LANES)])
        put_kv(N, p, block[:, :LANES], block[:, LANES:])

    forward([(p, N - 1) for p in range(PAIRS)])


    for c in [cp, ce, cr] + cc:
        c.wait()
    acc_d[...] = jnp.zeros_like(acc_d)
    acc_ff[...] = jnp.zeros_like(acc_ff)
    live_row = lax.broadcasted_iota(jnp.int32, (T, D), 0)

    def hidden_of(j):
        blended = jnp.concatenate([bl[p, live_rows_of(j), :] for p in range(PAIRS)], axis=1)
        return x[j].astype(f32) + dot(blended, wp[...]) + proj_bias

    def mlp(i, carry):
        frames = [i * MLP_FRAMES + t for t in range(MLP_FRAMES)]
        units = [(t, c) for c in range(FF // CHUNK) for t in range(MLP_FRAMES)]
        state = []
        for j in frames:
            scaled, inverse = normalise(hidden_of(j))
            second = (scaled * mlp_gain + mlp_shift).astype(bf16)
            sec[live_rows_of(j), :] = second
            upstream = jnp.where(live_row < limit(j), up0[j].astype(f32), 0.0)
            up_low = upstream.astype(bf16)
            up[live_rows_of(j), :] = up_low
            acc_d[pl.ds(0, 1), :] += column_sum(upstream)
            state.append((scaled, inverse, second, upstream, up_low))

        def products(t, c):
            cols = pl.ds(c * CHUNK, CHUNK)
            return dot(state[t][2], we[:, cols]), dot(state[t][4], wr[cols, :], NT)

        now = products(*units[0])
        grad_second = [None] * MLP_FRAMES
        for at, (t, c) in enumerate(units):
            later = products(*units[at + 1]) if at + 1 < len(units) else None
            j = frames[t]
            cols = pl.ds(c * CHUNK, CHUNK)
            gelu, slope = gelu_parts(now[0] + expand_bias[:, c * CHUNK:(c + 1) * CHUNK])
            a[live_rows_of(j), cols] = gelu.astype(bf16)
            grad_low = (now[1] * slope).astype(bf16)
            for b in range(CHUNK // LANES):
                base = pl.multiple_of((c * (CHUNK // LANES) + b) * R + j * F, 16)
                ge[pl.ds(base, T), :] = grad_low[:, b * LANES:(b + 1) * LANES]
            acc_ff[:, cols] += column_sum(grad_low.astype(f32))
            part = dot(grad_low, we[:, cols], NT)
            grad_second[t] = part if grad_second[t] is None else grad_second[t] + part
            now = later
        for t, j in enumerate(frames):
            scaled, inverse, second, upstream, up_low = state[t]
            acc_d[pl.ds(1, 1), :] += column_sum(grad_second[t] * scaled)
            acc_d[pl.ds(2, 1), :] += column_sum(grad_second[t])
            grad_hidden = upstream + norm_back(grad_second[t], scaled, inverse, mlp_gain)
            branch = grad_hidden.astype(bf16)
            gb[live_rows_of(j), :] = branch
            acc_d[pl.ds(3, 1), :] += column_sum(branch.astype(f32))
            grad_blended = (dot(branch, wp[...], NT).astype(bf16).astype(f32) * gh[j]).astype(bf16)
            gh[j] = grad_hidden
            for p in range(PAIRS):
                gbl[p, live_rows_of(j), :] = grad_blended[:, p * LANES:(p + 1) * LANES]
        return carry

    lax.fori_loop(0, N // MLP_FRAMES, mlp, 0)

    def pack(ref, base, block):
        block = block.astype(bf16)
        for t in range(block.shape[1] // LANES):
            ref[pl.ds(base + t * D, D), :] = block[:, t * LANES:(t + 1) * LANES]

    def pack_vectors(ref, base, rows, vectors):
        pieces = [w[:, t * LANES:(t + 1) * LANES] for w in vectors for t in range(w.shape[1] // LANES)]
        pieces.append(jnp.zeros((rows - len(pieces), LANES), f32))
        ref[pl.ds(base, rows), :] = jnp.concatenate(pieces, axis=0).astype(bf16)

    def big_weights(c, carry):
        cols = pl.ds(pl.multiple_of(c * D, LANES), D)
        base = pl.multiple_of(c * 3 * D, 16)
        pack(early, base, dot(sec[...], jnp.concatenate([ge[pl.ds(pl.multiple_of((c * 3 + t) * R, 16), R), :] for t in range(3)], axis=1), TN))
        pack(early, base + 12 * D, dot(up[...], a[:, cols], TN))
        return carry

    lax.fori_loop(0, FF // D, big_weights, 0)
    blended = jnp.concatenate([bl[p] for p in range(PAIRS)], axis=1)
    pack(early, 24 * D, dot(blended, gb[...], TN))
    pack_vectors(
        early, 27 * D, EARLY - 27 * D,
        [acc_d[pl.ds(0, 1), :], acc_ff[...], acc_d[pl.ds(1, 1), :], acc_d[pl.ds(2, 1), :], acc_d[pl.ds(3, 1), :]],
    )
    jobs[0].step(0)

    sums_ref = acc_d

    def lanes_of(i):
        return pl.ds(pl.multiple_of(i * LANES, LANES), LANES)

    def cols_of(p):
        return pl.ds(pl.multiple_of(p * D, LANES), D)

    def edge_rows(p, t):
        return pl.ds(pl.multiple_of(EARLY + p * 2 * F + t * F, 16), F)

    def edge(p):
        return pltpu.make_async_remote_copy(
            src_ref=ge.at[pl.ds(pl.multiple_of(EARLY + p * 2 * F, 16), 2 * F), :], dst_ref=hrecv.at[p], send_sem=hsem.at[2 + p],
            recv_sem=hsem.at[5 + p], device_id={"frame": other}, device_id_type=MESH,
        )

    def backward(p, carry):
        order = [(j, h) for j in (3, 2, 1, 0) for h in range(2)]
        prepared = {}

        def prepare(j):
            at = pl.ds(j * F, F)
            g = gbl[p, at, :]
            product = g.astype(f32) * (-bl[p, at, :].astype(f32))
            high = product.astype(bf16)
            rest = pltpu.roll(product - high.astype(f32), 64, 1).astype(bf16)
            return g, high, rest

        def grad_weights(j, h):
            if j not in prepared:
                prepared[j] = prepare(j)
            g, high, rest = prepared[j]
            extra = jnp.where(low, high, rest) if h == 0 else jnp.where(low, rest, high)
            return dot(jnp.concatenate([half(g, h), extra], axis=1), values_at(p, j), NT)

        sums = {}

        def add(s, part):
            sums[s] = part if s not in sums else [y + w for y, w in zip(sums[s], part)]

        dp = grad_weights(*order[0])
        scores = []
        queries = []
        for i, (j, h) in enumerate(order):
            later = grad_weights(*order[i + 1]) if i + 1 < len(order) else None
            ds = (dp * weights_at(p, j, h)[...].astype(f32)).astype(bf16)
            scores.append(ds)
            queries.append(dot(ds, k[p, span(j), :]))
            if h == 1:
                at = pl.ds(j * F, F)
                gj[p, at, pl.ds(0, LANES)] = (jnp.where(low, queries[0], queries[1]) * 0.125).astype(bf16)
                qq = q[p, at, :]
                g = prepared[j][0]
                dk = dot(
                    jnp.concatenate([half(qq, 0), half(qq, 1)], axis=0), jnp.concatenate(scores, axis=0), TN
                ).T
                both = e0[p] if j == 0 else e[p * 3 + j - 1]
                dv = dot(jnp.concatenate([half(g, 0), half(g, 1)], axis=0), both, TN).T
                for t, s in enumerate(window(j)):
                    add(s, [dk[t * F:(t + 1) * F], dv[t * F:(t + 1) * F]])
                scores, queries = [], []
                if j == 3:
                    ge[edge_rows(p, 0), :] = sums[N][0].astype(bf16)
                    ge[edge_rows(p, 1), :] = sums[N][1].astype(bf16)
                    edge(p).start()
            dp = later
        for s in range(N):
            for t in range(2):
                gj[p, pl.ds(s * F, F), pl.ds((1 + t) * LANES, LANES)] = sums[s][t].astype(bf16)
        columns = gj[p]
        outer = jnp.concatenate([ge[edge_rows(p, t), :] for t in range(2)], axis=1)
        outer_moment = dot(nh[...], outer, TN)
        moment = dot(n[...], columns, TN)
        moment = jnp.concatenate([moment[:, :LANES], moment[:, LANES:] + outer_moment], axis=1)
        summed = column_sum(columns.astype(f32))
        outer_sum = column_sum(outer.astype(f32))
        summed = jnp.concatenate([summed[:, :LANES], summed[:, LANES:] + outer_sum], axis=1)

        def put(group, first):
            job = jobs[1 + group]
            pack(job.src, pl.multiple_of((p - first) * 3 * D, 16), moment)
            sums_ref[pl.ds(p, 1), :] = summed

        def send(group):
            pairs = LATES[group]
            base = len(pairs) * 3 * D
            pack_vectors(jobs[1 + group].src, base, LATE[group] - base, [sums_ref[pl.ds(i, 1), :] for i in pairs])
            jobs[1 + group].step(0)

        @pl.when(p == 0)
        def _():
            put(0, 0)

        @pl.when(p == 1)
        def _():
            put(0, 0)
            send(0)

        @pl.when(p == 2)
        def _():
            put(1, 2)
            send(1)
            jobs[1].step(1)

        for i in range(PAIRS):
            @pl.when(p == i)
            def _():
                jobs[0].step(i + 1)

        return carry

    lax.fori_loop(0, PAIRS, backward, 0)

    def settle():
        for p in range(PAIRS):
            edge(p).wait()
            for t in range(2):
                at, cols = pl.ds(3 * F, F), pl.ds((1 + t) * LANES, LANES)
                gj[p, at, cols] = (gj[p, at, cols].astype(f32) + hrecv[p, pl.ds(t * F, F), :].astype(f32)).astype(bf16)

    def tail(finish):
        E, A, B = jobs
        finish(0, 0)
        B.step(1)
        finish(1, 0)
        A.step(2)
        E.step(4)
        finish(2, 0)
        B.step(2)
        settle()
        finish(3, 0)
        A.step(3)
        E.step(5)
        output(0)
        output(1)
        B.step(3)
        output(2)
        output(3)
        A.step(4)
        ordered = jnp.stack([up0[place(i)] for i in range(N)], axis=0)
        act_t[...] = jnp.swapaxes(ordered, 0, 1)
        pltpu.make_async_copy(act_t, act_out.at[0], osem.at[0]).start()
        B.step(4)
        E.step(6)
        A.step(5)
        B.step(5)
        A.step(6)
        E.step(7)
        B.step(6)

    def output(j):
        out = hidden_of(j) + dot(a[live_rows_of(j), :], wr[...]) + reduce_bias
        up0[j] = out.astype(bf16)

    def finish(j, carry):
        grad_normed = dot(jnp.concatenate([gj[p, live_rows_of(j), :] for p in range(PAIRS)], axis=1), wq[...], NT)
        scaled, inverse = normalise(x[j].astype(f32))
        gh[j] = gh[j] + norm_back(grad_normed, scaled, inverse, attn_gain)
        pltpu.make_async_copy(gh.at[j], grad_out.at[0, :, place(j), :], osem.at[4 + j]).start()
        return carry

    tail(finish)
    for i, job in enumerate(jobs):
        copy = pltpu.make_async_copy(job.fin.at[pl.ds(job.offset, job.rows)], outs[i], osem.at[8 + i])
        copy.start()
    for j in range(N):
        pltpu.make_async_copy(gh.at[j], grad_out.at[0, :, place(j), :], osem.at[4 + j]).wait()
    pltpu.make_async_copy(act_t, act_out.at[0], osem.at[0]).wait()
    for i, job in enumerate(jobs):
        pltpu.make_async_copy(job.fin.at[pl.ds(job.offset, job.rows)], outs[i], osem.at[8 + i]).wait()


def run_main(tokens, cot, w_qkv, w_proj, w_expand, w_reduce, *rest):
    hbm = pl.BlockSpec(memory_space=pl.ANY)
    vmem = pl.BlockSpec(memory_space=pltpu.VMEM)
    smem = pl.BlockSpec(memory_space=pltpu.SMEM)
    V = pltpu.VMEM
    scratch = [
        V((N + 1, T, D), bf16), V((N, T, D), bf16), V((D, 3 * D), bf16), V((D, D), bf16), V((D, FF), bf16), V((FF, D), bf16),
        V((R, D), bf16), V((F, D), bf16), V((PAIRS, R, LANES), bf16), V((PAIRS, R + F, LANES), bf16), V((PAIRS, R + F, LANES), bf16),
        V((PAIRS, 2 * F, 2 * F), bf16), V((PAIRS * 3, 2 * F, 3 * F), bf16),
        V((PAIRS, R, LANES), bf16),
        V((3, R, D), bf16), V((R, FF), bf16), V((FF // LANES * R, LANES), bf16), V((N, T, D), f32),
        V((PAIRS, R, LANES), bf16),
        V((PAIRS, 2 * F, LANES), bf16), V((T, N, D), bf16), V((8, D), f32), V((1, FF), f32),
        pltpu.SemaphoreType.DMA((24,)), pltpu.SemaphoreType.DMA((11,)), pltpu.SemaphoreType.DMA((8,)),
    ] + Sum.scratch(EARLY, True) + Sum.scratch(LATE[0], False) + [V((LATE[1], LANES), bf16)] + Sum.scratch(LATE[1], False)
    return pl.pallas_call(
        main_kernel,
        out_shape=[
            jax.ShapeDtypeStruct((1, T, N, D), bf16), jax.ShapeDtypeStruct((1, T, N, D), f32),
            jax.ShapeDtypeStruct((EARLY, LANES), bf16), jax.ShapeDtypeStruct((LATE[0], LANES), bf16),
            jax.ShapeDtypeStruct((LATE[1], LANES), bf16),
        ],
        in_specs=[hbm] * 6 + [vmem] * 9 + [smem] * 2,
        out_specs=[hbm] * 5,
        scratch_shapes=scratch,
        compiler_params=pltpu.CompilerParams(
            collective_id=0, has_side_effects=True, vmem_limit_bytes=66_500_000
        ),
    )(tokens, cot, w_qkv, w_proj, w_expand, w_reduce, *rest)


def final_kernel(
    early_in, late0_in, late1_in, wq_in, gain_ref, shift_ref, act_in, grad_in,
    o_ag, o_as, o_wq, o_qb, o_vb, o_wp, o_pb, o_mg, o_ms, o_we, o_eb, o_wr, o_rb, o_norm, o_act, o_grad,
    early, late0, late1, wq, s_wq, s_wp, s_we, s_wr, s_act, s_grad, isem, osem,
):
    half = 12 * D
    pieces = [
        (early_in.at[pl.ds(half, half)], early.at[pl.ds(half, half)]), (early_in.at[pl.ds(0, half)], early.at[pl.ds(0, half)]),
        (early_in.at[pl.ds(2 * half, EARLY - 2 * half)], early.at[pl.ds(2 * half, EARLY - 2 * half)]),
        (late0_in, late0), (late1_in, late1), (wq_in, wq),
    ]
    fetches = [pltpu.make_async_copy(src, dst, isem.at[i]) for i, (src, dst) in enumerate(pieces)]
    for copy in fetches:
        copy.start()

    whole = [pltpu.make_async_copy(act_in, s_act, isem.at[6]), pltpu.make_async_copy(grad_in, s_grad, isem.at[7])]
    for copy in whole:
        copy.start()

    def square(total, block):
        return total + jnp.sum(block * block, axis=0, keepdims=True)

    total = jnp.zeros((1, LANES), f32)
    stores = []

    def store(src, dst):
        copy = pltpu.make_async_copy(src, dst, osem.at[len(stores)])
        copy.start()
        stores.append(copy)

    fetches[0].wait()
    for c in range(12):
        block = early[pl.ds(half + c * D, D), :].astype(f32)
        s_wr[pl.ds(c * LANES, LANES), :] = block.T
        total = square(total, block)
    store(s_wr, o_wr)
    whole[0].wait()
    store(s_act, o_act)
    whole[1].wait()
    store(s_grad, o_grad)
    fetches[1].wait()
    for c in range(12):
        block = early[pl.ds(c * D, D), :].astype(f32)
        s_we[:, pl.ds(c * LANES, LANES)] = block
        total = square(total, block)
    store(s_we, o_we)
    fetches[2].wait()
    for c in range(3):
        block = early[pl.ds(2 * half + c * D, D), :].astype(f32)
        s_wp[:, pl.ds(c * LANES, LANES)] = block
        total = square(total, block)
    store(s_wp, o_wp)
    tail = early[pl.ds(27 * D, 32), :].astype(f32)
    total = square(total, tail[:24])
    lines = [tail[i:i + 1] for i in range(24)]

    def line(parts):
        return jnp.concatenate(parts, axis=1).reshape(len(parts) * LANES)

    o_rb[...] = line(lines[:3])
    o_eb[...] = line(lines[3:15])
    o_mg[...] = line(lines[15:18])
    o_ms[...] = line(lines[18:21])
    o_pb[...] = line(lines[21:24])

    def column(ref):
        row = ref[...].reshape(1, D)
        return jnp.broadcast_to(row, (LANES, D)).T

    gain, shift = column(gain_ref), column(shift_ref)
    for copy in fetches[3:]:
        copy.wait()
    along_gain = jnp.zeros((D, LANES), f32)
    along_shift = jnp.zeros((D, LANES), f32)
    sums = {}
    for group, ref in ((0, late0), (1, late1)):
        pairs = LATES[group]
        extra = ref[pl.ds(len(pairs) * 3 * D, 16), :].astype(f32)
        for i, p in enumerate(pairs):
            for t in range(3):
                moment = ref[pl.ds((i * 3 + t) * D, D), :].astype(f32)
                summed = extra[i * 3 + t:i * 3 + t + 1]
                sums[t, p] = summed
                cols = pl.ds((t * PAIRS + p) * LANES, LANES)
                weight = wq[:, cols].astype(f32)
                block = gain * moment + shift * summed
                s_wq[:, cols] = block
                total = square(total, block)
                along_gain = along_gain + weight * moment
                along_shift = along_shift + weight * summed
    store(s_wq, o_wq)
    grad_gain = jnp.sum(along_gain.T, axis=0, keepdims=True)
    grad_shift = jnp.sum(along_shift.T, axis=0, keepdims=True)
    o_ag[...] = grad_gain.reshape(D)
    o_as[...] = grad_shift.reshape(D)
    o_qb[...] = line([sums[0, p] for p in range(PAIRS)])
    o_vb[...] = line([sums[2, p] for p in range(PAIRS)])
    for p in range(PAIRS):
        total = square(square(total, sums[0, p]), sums[2, p])
        cols = slice(p * LANES, (p + 1) * LANES)
        total = square(square(total, grad_gain[:, cols]), grad_shift[:, cols])
    o_norm[...] = jnp.sqrt(jnp.sum(total, axis=1, keepdims=True))
    for copy in stores:
        copy.wait()


def run_final(early, late0, late1, w_qkv, gain, shift, act, grad):
    hbm = pl.BlockSpec(memory_space=pl.ANY)
    vmem = pl.BlockSpec(memory_space=pltpu.VMEM)
    V = pltpu.VMEM
    vector = jax.ShapeDtypeStruct((D,), f32)

    def matrix(a, b):
        return jax.ShapeDtypeStruct((a, b), f32)

    shapes = [
        vector, vector, matrix(D, 3 * D), vector, vector, matrix(D, D), vector, vector, vector, matrix(D, FF),
        jax.ShapeDtypeStruct((FF,), f32), matrix(FF, D), vector, matrix(1, 1),
        jax.ShapeDtypeStruct(act.shape, act.dtype), jax.ShapeDtypeStruct(grad.shape, grad.dtype),
    ]
    return pl.pallas_call(
        final_kernel,
        out_shape=shapes,
        in_specs=[hbm] * 4 + [vmem] * 2 + [hbm] * 2,
        out_specs=[hbm if len(s.shape) > 1 and s.shape[-1] > 1 else vmem for s in shapes],
        scratch_shapes=[
            V((EARLY, LANES), bf16), V((LATE[0], LANES), bf16), V((LATE[1], LANES), bf16), V((D, 3 * D), bf16),
            V((D, 3 * D), f32), V((D, D), f32), V((D, FF), f32), V((FF, D), f32),
            V(act.shape, bf16), V(grad.shape, f32),
            pltpu.SemaphoreType.DMA((8,)), pltpu.SemaphoreType.DMA((6,)),
        ],
        compiler_params=pltpu.CompilerParams(vmem_limit_bytes=66_500_000),
    )(early, late0, late1, w_qkv, gain, shift, act, grad)


def body(
    tokens, attn_gain, attn_shift, w_qkv, query_bias, value_bias, w_proj, proj_bias, mlp_gain, mlp_shift,
    w_expand, expand_bias, w_reduce, reduce_bias, cotangent, resolution, frame_count,
):
    act, grad, early, late0, late1 = run_main(
        tokens, cotangent, w_qkv, w_proj, w_expand, w_reduce, attn_gain, attn_shift, query_bias, value_bias,
        proj_bias, mlp_gain, mlp_shift, reduce_bias, expand_bias, resolution, frame_count,
    )
    *grads, norm, act, grad = run_final(early, late0, late1, w_qkv, attn_gain, attn_shift, act, grad)
    return (jnp.transpose(act, (0, 2, 1, 3)), jnp.transpose(grad, (0, 2, 1, 3)), *grads, norm.reshape(()))


def solution(mesh):
    data = P("clip", "frame", None, None)
    return jax.shard_map(
        body,
        mesh=mesh,
        in_specs=(data,) + (P(),) * 13 + (data, P("clip"), P("clip")),
        out_specs=(data, data) + (P(),) * 14,
        check_vma=False,
    )
```

```python
import functools
import jax
import jax.numpy as jnp
from jax import lax
from jax.sharding import PartitionSpec as P
from jax.experimental import pallas as pl
from jax.experimental.pallas import tpu as pltpu

T = 324
F = 336
D = 384
FF = 1536
N = 4
PAIRS = 3
EPS = 1e-6
NEG = -1e9
PAD = -1e30
LANES = 128
CHUNK = 256
MLP_FRAMES = 2
R = N * F
f32 = jnp.float32
bf16 = jnp.bfloat16
NT = (((1,), (1,)), ((), ()))
NN = (((1,), (0,)), ((), ()))
TN = (((0,), (0,)), ((), ()))
MESH = pl.DeviceIdType.MESH


def dot(a, b, dims=NN):
    return lax.dot_general(a, b, dims, preferred_element_type=f32)


def rows_of(slot):
    return pl.ds(pl.multiple_of(slot * F, 16), F)


def live_rows_of(slot):
    return pl.ds(pl.multiple_of(slot * F, 16), T)


def normalise(x):
    centre = x - jnp.mean(x, axis=1, keepdims=True)
    spread = jnp.mean(centre * centre, axis=1, keepdims=True)
    inverse = lax.rsqrt(spread + EPS)
    return centre * inverse, inverse


def norm_back(grad, scaled, inverse, gain):
    e = grad * gain
    return inverse * (
        e - jnp.mean(e, axis=1, keepdims=True) - scaled * jnp.mean(e * scaled, axis=1, keepdims=True)
    )


def gelu_parts(x):
    u = jnp.exp(-0.5 * (x * x))
    t = 1.0 / (1.0 + 0.23164188844 * jnp.abs(x))
    p = t * (0.127414796 + t * (-0.142248368 + t * (0.7107068705 + t * (-0.7265760135 + t * 0.5307027145))))
    h = p * u
    cdf = jnp.where(x >= 0, 1.0 - h, h)
    return x * cdf, cdf + x * (u * 0.3989422804014327)


def column_sum(x):
    return jnp.sum(x, axis=0, keepdims=True)


def coordinates():
    clip = lax.axis_index("clip")
    z_hi = lax.axis_index("frame")
    core = clip % 2
    x = (clip // 2) % 4
    z_lo = (clip // 8) % 2
    y = clip // 16
    return x, y, 2 * z_hi + z_lo, core


def device_at(x, y, z, core):
    return {"clip": ((y * 2 + z % 2) * 4 + x) * 2 + core, "frame": z // 2}


def along(axis, step):
    x, y, z, core = coordinates()
    if axis == 0:
        x = (x + step) % 4
    elif axis == 1:
        y = (y + step) % 4
    else:
        z = (z + step) % 4
    return device_at(x, y, z, core)


def across():
    x, y, z, core = coordinates()
    return device_at(x, y, z, 1 - core)


def enter():
    barrier = pltpu.get_barrier_semaphore()
    pl.semaphore_signal(barrier, inc=1, device_id=across(), device_id_type=MESH)
    for axis in range(3):
        for step in (1, 2, 3):
            pl.semaphore_signal(barrier, inc=1, device_id=along(axis, step), device_id_type=MESH)


def entered():
    pl.semaphore_wait(pltpu.get_barrier_semaphore(), 10)


def total_of(parts):
    out = parts[0].astype(f32)
    for part in parts[1:]:
        out = out + part.astype(f32)
    return out.astype(bf16)


def strip(base, rows):
    return pl.ds(pl.multiple_of(base, 16), rows)


class Sum:
    def __init__(self, rows, scatter, fin, offset, src, rcore, r1, w1, r2, w2, r3, sems):
        self.rows, self.scatter, self.offset = rows, scatter, offset
        self.src, self.fin, self.rcore, self.r1, self.w1, self.r2, self.w2, self.r3, self.sems = (
            src, fin, rcore, r1, w1, r2, w2, r3, sems)
        self.half, self.part, self.chunk = rows // 2, rows // 6, rows // 24
        self.sub = rows // 96 if scatter else rows // 24

    @staticmethod
    def scratch(rows, scatter):
        sub = rows // 96 if scatter else rows // 24
        return [
            pltpu.VMEM((rows, LANES), bf16), pltpu.VMEM((rows // 2, LANES), bf16),
            pltpu.VMEM((3, 3, rows // 24, LANES), bf16), pltpu.VMEM((3, rows // 24, LANES), bf16),
            pltpu.VMEM((3, 3, sub, LANES) if scatter else (3, 4, sub, LANES), bf16), pltpu.VMEM((3, sub, LANES), bf16),
            pltpu.VMEM((3, 4, sub, LANES), bf16),
            pltpu.SemaphoreType.DMA((2, 2 + 9 * (5 if scatter else 4))),
        ]

    def spot(self, part, level):
        return coordinates()[(part + level) % 3]

    def home(self, part, level):
        base = coordinates()[3] * self.half + part * self.part
        if level >= 1:
            base = base + self.spot(part, 0) * self.chunk
        if level >= 2 and self.scatter:
            base = base + self.spot(part, 1) * self.sub
        return base

    def copies(self, stage):
        core = coordinates()[3]
        out = []
        last = 6 if self.scatter else 5
        if stage == 0:
            out.append((self.src.at[strip((1 - core) * self.half, self.half)], self.rcore, across()))
        elif stage == last:
            here = self.fin.at[strip(self.offset + core * self.half, self.half)]
            out.append((here, here, across()))
        else:
            for part in range(3):
                for step in (1, 2, 3):
                    if stage == 1:
                        target = self.home(part, 0) + (self.spot(part, 0) + step) % 4 * self.chunk
                        out.append((self.src.at[strip(target, self.chunk)], self.r1.at[part, step - 1], along(part, step)))
                    elif stage == 2 and self.scatter:
                        target = (self.spot(part, 1) + step) % 4 * self.sub
                        out.append((self.w1.at[part, strip(target, self.sub)], self.r2.at[part, step - 1], along((part + 1) % 3, step)))
                    elif stage == 2:
                        out.append((self.w1.at[part], self.r2.at[part, self.spot(part, 1)], along((part + 1) % 3, step)))
                    elif stage == 3:
                        out.append((self.w2.at[part], self.r3.at[part, self.spot(part, 2)], along((part + 2) % 3, step)))
                    else:
                        axis, level, rows = (1, 2, self.sub) if self.scatter and stage == 4 else (0, 1, self.chunk)
                        here = self.fin.at[strip(self.offset + self.home(part, level), rows)]
                        out.append((here, here, along((part + axis) % 3, step)))
        first = 0 if stage == 0 else 1 + 9 * (stage - 1)
        return [
            pltpu.make_async_remote_copy(
                src_ref=src, dst_ref=dst, send_sem=self.sems.at[0, first + i], recv_sem=self.sems.at[1, first + i],
                device_id=device, device_id_type=MESH,
            )
            for i, (src, dst, device) in enumerate(out)
        ]

    def start(self, stage):
        for copy in self.copies(stage):
            copy.start()

    def arrive(self, stage):
        for copy in self.copies(stage):
            copy.wait()

    def step(self, stage):
        last = 6 if self.scatter else 5
        if stage > last + 1:
            return
        if stage > 0:
            self.arrive(stage - 1)
        if stage == 1:
            mine = strip(coordinates()[3] * self.half, self.half)
            self.src[mine, :] = total_of([self.src[mine, :], self.rcore[...]])
        for part in range(3):
            if stage == 2:
                own = self.src[strip(self.home(part, 1), self.chunk), :]
                total = total_of([own] + [self.r1[part, i] for i in range(3)])
                self.w1[part] = total
                if not self.scatter:
                    self.r2[part, self.spot(part, 1)] = total
            elif stage == 3:
                if self.scatter:
                    own = self.w1[part, strip(self.spot(part, 1) * self.sub, self.sub), :]
                    total = total_of([own] + [self.r2[part, i] for i in range(3)])
                else:
                    total = total_of([self.r2[part, i] for i in range(4)])
                self.w2[part] = total
                self.r3[part, self.spot(part, 2)] = total
            elif stage == 4:
                here = strip(self.offset + self.home(part, 2), self.sub)
                self.fin[here, :] = total_of([self.r3[part, i] for i in range(4)])
        if stage <= last:
            self.start(stage)


FIRST = 4608
SECOND = 6144
EARLY = 10752
LATES = ((0, 1), (2,))
LATE = tuple(-(-(len(g) * 9 * LANES + 16) // 384) * 384 for g in LATES)


def main_kernel(
    tokens, cot, w_qkv, w_proj, w_expand, w_reduce,
    v_ag, v_as, v_qb, v_vb, v_pb, v_mg, v_ms, v_rb, v_eb, res, cnt,
    act_out, grad_out, early_out, late0_out, late1_out,
    x, up0, wq, wp, we, wr, n, nh, q, k, v, e0, e, bl, trio, a, ge, gh, gbl, hrecv, act_t,
    acc_d, acc_ff, lsem, osem, hsem, *rest,
):
    z = lax.axis_index("frame")
    sec, up, gb = trio.at[0], trio.at[1], trio.at[2]
    gj = trio
    jobs = [Sum(FIRST, True, ge, 0, *rest[:8]), Sum(LATE[0], False, ge, EARLY + PAIRS * 2 * F, *rest[8:16]), Sum(LATE[1], False, rest[16], 0, *rest[17:25]),
            Sum(SECOND, True, ge, FIRST, *rest[25:33])]
    outs = [early_out.at[pl.ds(0, FIRST)], late0_out, late1_out, early_out.at[pl.ds(FIRST, SECOND)]]
    other = 1 - z

    def place(s):
        return s + z * (3 - 2 * s)

    local = []

    def fetch(src, dst):
        c = pltpu.make_async_copy(src, dst, lsem.at[len(local)])
        c.start()
        local.append(c)
        return c

    cx = [fetch(tokens.at[0, place(s)], x.at[s]) for s in range(N)]
    cq = [
        fetch(w_qkv.at[:, pl.ds((t * PAIRS + p) * LANES, LANES)], wq.at[:, pl.ds((p * 3 + t) * LANES, LANES)])
        for p in range(PAIRS) for t in range(3)
    ]
    enter()
    cp = fetch(w_proj, wp)
    ce = fetch(w_expand, we)
    cr = fetch(w_reduce, wr)
    cc = [fetch(cot.at[0, place(s)], up0.at[s]) for s in range(N)]

    attn_gain, attn_shift, query_bias, value_bias, proj_bias, mlp_gain, mlp_shift, reduce_bias, expand_bias = [
        ref[...].astype(f32).reshape(1, ref.shape[0])
        for ref in (v_ag, v_as, v_qb, v_vb, v_pb, v_mg, v_ms, v_rb, v_eb)
    ]

    def limit(s):
        frame = s + z * (7 - 2 * s)
        return jnp.where(frame < cnt[0], res[0], 0)

    for ref in (n, nh, sec, up, a, gb, *[q.at[p] for p in range(PAIRS)]):
        for s in range(ref.shape[0] // F):
            ref[pl.ds(s * F + T, F - T), :] = jnp.zeros((F - T, ref.shape[1]), ref.dtype)
    for p in range(PAIRS):
        for s in range(N):
            gbl[p, pl.ds(s * F + T, F - T), :] = jnp.zeros((F - T, LANES), bf16)
        for s in range(N + 1):
            k[p, pl.ds(s * F + T, F - T), :] = jnp.zeros((F - T, LANES), bf16)
            v[p, pl.ds(s * F + T, F - T), :] = jnp.zeros((F - T, LANES), bf16)
    for t in range(FF // LANES * N):
        ge[pl.ds(t * F + T, F - T), :] = jnp.zeros((F - T, LANES), bf16)
    row = lax.broadcasted_iota(jnp.int32, (F, LANES), 0)
    lane = lax.broadcasted_iota(jnp.int32, (F, LANES), 1)
    low = lane < 64

    def put_kv(s, p, keys, values):
        k[p, live_rows_of(s), :] = jnp.where(row[:T] < limit(s), keys, 0.0).astype(bf16)
        v[p, live_rows_of(s), :] = (values + value_bias[:, p * LANES:(p + 1) * LANES]).astype(bf16)

    for c in cx + cq:
        c.wait()

    def project(s, carry):
        scaled, _ = normalise(x[s].astype(f32))
        n[live_rows_of(s), :] = scaled.astype(bf16)
        joined = dot((scaled * attn_gain + attn_shift).astype(bf16), wq[...])
        for p in range(PAIRS):
            block = joined[:, p * D:(p + 1) * D]
            biased = (block[:, :LANES] + query_bias[:, p * LANES:(p + 1) * LANES]).astype(bf16)
            q[p, live_rows_of(s), :] = biased * jnp.asarray(0.125, bf16)
            put_kv(s, p, block[:, LANES:2 * LANES], block[:, 2 * LANES:])
        return carry

    lax.fori_loop(0, N, project, 0)

    entered()
    halo = pltpu.make_async_remote_copy(
        src_ref=tokens.at[0, place(N - 1)], dst_ref=x.at[N], send_sem=hsem.at[0], recv_sem=hsem.at[1],
        device_id={"frame": other}, device_id_type=MESH,
    )
    halo.start()

    def window(j):
        return list(range(max(j - 1, 0), j + 2))

    def span(j):
        w = window(j)
        return pl.ds(w[0] * F, len(w) * F)

    def bias_of(j):
        w = window(j)
        at = lax.broadcasted_iota(jnp.int32, (1, len(w) * F), 1)
        out = jnp.zeros((1, len(w) * F), f32)
        for i, s in enumerate(w):
            inside = (at >= i * F) & (at < (i + 1) * F)
            out = jnp.where(inside & (at >= i * F + limit(s)), NEG, out)
            out = jnp.where(inside & (at >= i * F + T), PAD, out)
        return out

    def half(value, h):
        zero = jnp.zeros_like(value)
        return jnp.where(low, value, zero) if h == 0 else jnp.where(low, zero, value)

    def values_at(p, j):
        return jnp.concatenate([v[p, span(j), :], jnp.ones((len(window(j)) * F, LANES), bf16)], axis=1)

    def weights_at(p, j, h):
        if j == 0:
            return e0.at[p, pl.ds(h * F, F)]
        return e.at[p * 3 + j - 1, pl.ds(h * F, F)]

    def forward(units):
        order = [(p, j, h) for p, j in units for h in range(2)]

        def scores(p, j, h):
            return dot(half(q[p, pl.ds(j * F, F), :], h), k[p, span(j), :], NT) + bias_of(j)

        s = scores(*order[0])
        held = []
        for i, (p, j, h) in enumerate(order):
            later = scores(*order[i + 1]) if i + 1 < len(order) else None
            largest = jnp.max(s, axis=1, keepdims=True)
            ex = jnp.exp(s - largest).astype(bf16)
            weights_at(p, j, h)[...] = ex
            o = dot(ex, values_at(p, j))
            total = o[:, LANES:]
            if j == 0:
                total = total + T * jnp.exp(NEG - largest)
            held.append((o[:, :LANES], 1.0 / total))
            if h == 1:
                (oa, ia), (ob, ib) = held
                held = []
                both = jnp.where(low, ia, ib)
                gh[j, :, pl.ds(pl.multiple_of(p * LANES, LANES), LANES)] = both[:T]
                bl[p, pl.ds(j * F, F), :] = (jnp.where(low, oa, ob) * both).astype(bf16)
            s = later

    def inner(p, carry):
        forward([(p, j) for j in range(N - 1)])
        return carry

    lax.fori_loop(0, PAIRS, inner, 0)
    halo.wait()
    scaled, _ = normalise(x[N].astype(f32))
    nh[pl.ds(0, T), :] = scaled.astype(bf16)
    normed = (scaled * attn_gain + attn_shift).astype(bf16)
    for p in range(PAIRS):
        block = dot(normed, wq[:, pl.ds(p * D + LANES, 2 * LANES)])
        put_kv(N, p, block[:, :LANES], block[:, LANES:])

    forward([(p, N - 1) for p in range(PAIRS)])


    for c in [cp, ce, cr] + cc:
        c.wait()
    acc_d[...] = jnp.zeros_like(acc_d)
    acc_ff[...] = jnp.zeros_like(acc_ff)
    live_row = lax.broadcasted_iota(jnp.int32, (T, D), 0)

    def hidden_of(j):
        blended = jnp.concatenate([bl[p, live_rows_of(j), :] for p in range(PAIRS)], axis=1)
        return x[j].astype(f32) + dot(blended, wp[...]) + proj_bias

    def mlp(i, carry):
        frames = [i * MLP_FRAMES + t for t in range(MLP_FRAMES)]
        units = [(t, c) for c in range(FF // CHUNK) for t in range(MLP_FRAMES)]
        state = []
        for j in frames:
            scaled, inverse = normalise(hidden_of(j))
            second = (scaled * mlp_gain + mlp_shift).astype(bf16)
            sec[live_rows_of(j), :] = second
            upstream = jnp.where(live_row < limit(j), up0[j].astype(f32), 0.0)
            up_low = upstream.astype(bf16)
            up[live_rows_of(j), :] = up_low
            acc_d[pl.ds(0, 1), :] += column_sum(upstream)
            state.append((scaled, inverse, second, upstream, up_low))

        def products(t, c):
            cols = pl.ds(c * CHUNK, CHUNK)
            return dot(state[t][2], we[:, cols]), dot(state[t][4], wr[cols, :], NT)

        now = products(*units[0])
        grad_second = [None] * MLP_FRAMES
        for at, (t, c) in enumerate(units):
            later = products(*units[at + 1]) if at + 1 < len(units) else None
            j = frames[t]
            cols = pl.ds(c * CHUNK, CHUNK)
            gelu, slope = gelu_parts(now[0] + expand_bias[:, c * CHUNK:(c + 1) * CHUNK])
            a[live_rows_of(j), cols] = gelu.astype(bf16)
            grad_low = (now[1] * slope).astype(bf16)
            for b in range(CHUNK // LANES):
                base = pl.multiple_of((c * (CHUNK // LANES) + b) * R + j * F, 16)
                ge[pl.ds(base, T), :] = grad_low[:, b * LANES:(b + 1) * LANES]
            acc_ff[:, cols] += column_sum(grad_low.astype(f32))
            part = dot(grad_low, we[:, cols], NT)
            grad_second[t] = part if grad_second[t] is None else grad_second[t] + part
            now = later
        for t, j in enumerate(frames):
            scaled, inverse, second, upstream, up_low = state[t]
            acc_d[pl.ds(1, 1), :] += column_sum(grad_second[t] * scaled)
            acc_d[pl.ds(2, 1), :] += column_sum(grad_second[t])
            grad_hidden = upstream + norm_back(grad_second[t], scaled, inverse, mlp_gain)
            branch = grad_hidden.astype(bf16)
            gb[live_rows_of(j), :] = branch
            acc_d[pl.ds(3, 1), :] += column_sum(branch.astype(f32))
            grad_blended = (dot(branch, wp[...], NT).astype(bf16).astype(f32) * gh[j]).astype(bf16)
            gh[j] = grad_hidden
            for p in range(PAIRS):
                gbl[p, live_rows_of(j), :] = grad_blended[:, p * LANES:(p + 1) * LANES]
        return carry

    lax.fori_loop(0, N // MLP_FRAMES, mlp, 0)

    def pack(ref, base, block):
        block = block.astype(bf16)
        for t in range(block.shape[1] // LANES):
            ref[pl.ds(base + t * D, D), :] = block[:, t * LANES:(t + 1) * LANES]

    def pack_vectors(ref, base, rows, vectors):
        pieces = [w[:, t * LANES:(t + 1) * LANES] for w in vectors for t in range(w.shape[1] // LANES)]
        pieces.append(jnp.zeros((rows - len(pieces), LANES), f32))
        ref[pl.ds(base, rows), :] = jnp.concatenate(pieces, axis=0).astype(bf16)

    first, second_job = jobs[0], jobs[3]

    def reduce_weights(c, carry):
        cols = pl.ds(pl.multiple_of(c * D, LANES), D)
        pack(first.src, pl.multiple_of(c * 3 * D, 16), dot(up[...], a[:, cols], TN))
        return carry

    lax.fori_loop(0, FF // D, reduce_weights, 0)
    first.step(0)

    def expand_weights(c, carry):
        tiles = [ge[pl.ds(pl.multiple_of((c * 3 + t) * R, 16), R), :] for t in range(3)]
        pack(second_job.src, pl.multiple_of(c * 3 * D, 16), dot(sec[...], jnp.concatenate(tiles, axis=1), TN))
        return carry

    lax.fori_loop(0, FF // D, expand_weights, 0)
    blended = jnp.concatenate([bl[p] for p in range(PAIRS)], axis=1)
    pack(second_job.src, 12 * D, dot(blended, gb[...], TN))
    pack_vectors(
        second_job.src, 15 * D, SECOND - 15 * D,
        [acc_d[pl.ds(0, 1), :], acc_ff[...], acc_d[pl.ds(1, 1), :], acc_d[pl.ds(2, 1), :], acc_d[pl.ds(3, 1), :]],
    )
    first.step(1)
    second_job.step(0)

    sums_ref = acc_d

    def lanes_of(i):
        return pl.ds(pl.multiple_of(i * LANES, LANES), LANES)

    def cols_of(p):
        return pl.ds(pl.multiple_of(p * D, LANES), D)

    def edge_rows(p, t):
        return pl.ds(pl.multiple_of(EARLY + p * 2 * F + t * F, 16), F)

    def edge(p):
        return pltpu.make_async_remote_copy(
            src_ref=ge.at[pl.ds(pl.multiple_of(EARLY + p * 2 * F, 16), 2 * F), :], dst_ref=hrecv.at[p], send_sem=hsem.at[2 + p],
            recv_sem=hsem.at[5 + p], device_id={"frame": other}, device_id_type=MESH,
        )

    def advance(p, sites):
        for i in range(PAIRS):
            @pl.when(p == i)
            def _():
                for job, stage in sites[i]:
                    job.step(stage)

    def backward(p, carry):
        order = [(j, h) for j in (3, 2, 1, 0) for h in range(2)]
        prepared = {}

        def prepare(j):
            at = pl.ds(j * F, F)
            g = gbl[p, at, :]
            product = g.astype(f32) * (-bl[p, at, :].astype(f32))
            high = product.astype(bf16)
            rest = pltpu.roll(product - high.astype(f32), 64, 1).astype(bf16)
            return g, high, rest

        def grad_weights(j, h):
            if j not in prepared:
                prepared[j] = prepare(j)
            g, high, rest = prepared[j]
            extra = jnp.where(low, high, rest) if h == 0 else jnp.where(low, rest, high)
            return dot(jnp.concatenate([half(g, h), extra], axis=1), values_at(p, j), NT)

        sums = {}

        def add(s, part):
            sums[s] = part if s not in sums else [y + w for y, w in zip(sums[s], part)]

        dp = grad_weights(*order[0])
        scores = []
        queries = []
        for i, (j, h) in enumerate(order):
            later = grad_weights(*order[i + 1]) if i + 1 < len(order) else None
            ds = (dp * weights_at(p, j, h)[...].astype(f32)).astype(bf16)
            scores.append(ds)
            queries.append(dot(ds, k[p, span(j), :]))
            if h == 1:
                at = pl.ds(j * F, F)
                gj[p, at, pl.ds(0, LANES)] = (jnp.where(low, queries[0], queries[1]) * 0.125).astype(bf16)
                qq = q[p, at, :]
                g = prepared[j][0]
                dk = dot(
                    jnp.concatenate([half(qq, 0), half(qq, 1)], axis=0), jnp.concatenate(scores, axis=0), TN
                ).T
                both = e0[p] if j == 0 else e[p * 3 + j - 1]
                dv = dot(jnp.concatenate([half(g, 0), half(g, 1)], axis=0), both, TN).T
                for t, s in enumerate(window(j)):
                    add(s, [dk[t * F:(t + 1) * F], dv[t * F:(t + 1) * F]])
                scores, queries = [], []
                if j == 3:
                    ge[edge_rows(p, 0), :] = sums[N][0].astype(bf16)
                    ge[edge_rows(p, 1), :] = sums[N][1].astype(bf16)
                    edge(p).start()
                if j == 2:
                    advance(p, [[(second_job, 1)], [(second_job, 2)], [(second_job, 3), (first, 4)]])
            dp = later
        for s in range(N):
            for t in range(2):
                gj[p, pl.ds(s * F, F), pl.ds((1 + t) * LANES, LANES)] = sums[s][t].astype(bf16)
        columns = gj[p]
        outer = jnp.concatenate([ge[edge_rows(p, t), :] for t in range(2)], axis=1)
        outer_moment = dot(nh[...], outer, TN)
        moment = dot(n[...], columns, TN)
        moment = jnp.concatenate([moment[:, :LANES], moment[:, LANES:] + outer_moment], axis=1)
        summed = column_sum(columns.astype(f32))
        outer_sum = column_sum(outer.astype(f32))
        summed = jnp.concatenate([summed[:, :LANES], summed[:, LANES:] + outer_sum], axis=1)

        def put(group, first):
            job = jobs[1 + group]
            pack(job.src, pl.multiple_of((p - first) * 3 * D, 16), moment)
            sums_ref[pl.ds(p, 1), :] = summed

        def send(group):
            pairs = LATES[group]
            base = len(pairs) * 3 * D
            pack_vectors(jobs[1 + group].src, base, LATE[group] - base, [sums_ref[pl.ds(i, 1), :] for i in pairs])
            jobs[1 + group].step(0)

        @pl.when(p == 0)
        def _():
            put(0, 0)

        @pl.when(p == 1)
        def _():
            put(0, 0)
            send(0)

        @pl.when(p == 2)
        def _():
            put(1, 2)
            send(1)
            jobs[1].step(1)

        advance(p, [[(first, 2)], [(first, 3)], [(second_job, 4), (first, 5)]])

        return carry

    lax.fori_loop(0, PAIRS, backward, 0)

    def settle():
        for p in range(PAIRS):
            edge(p).wait()
            for t in range(2):
                at, cols = pl.ds(3 * F, F), pl.ds((1 + t) * LANES, LANES)
                gj[p, at, cols] = (gj[p, at, cols].astype(f32) + hrecv[p, pl.ds(t * F, F), :].astype(f32)).astype(bf16)

    def tail(finish):
        E, A, B, G = jobs
        finish(0, 0)
        B.step(1)
        finish(1, 0)
        A.step(2)
        finish(2, 0)
        settle()
        G.step(5)
        B.step(2)
        finish(3, 0)
        E.step(6)
        output(0)
        A.step(3)
        output(1)
        output(2)
        B.step(3)
        output(3)
        A.step(4)
        E.step(7)
        leave(0)
        G.step(6)
        B.step(4)
        ordered = jnp.stack([up0[place(i)] for i in range(N)], axis=0)
        act_t[...] = jnp.swapaxes(ordered, 0, 1)
        pltpu.make_async_copy(act_t, act_out.at[0], osem.at[0]).start()
        A.step(5)
        G.step(7)
        leave(3)
        B.step(5)
        A.step(6)
        leave(1)
        B.step(6)
        leave(2)

    def result(i):
        job = jobs[i]
        return pltpu.make_async_copy(job.fin.at[pl.ds(job.offset, job.rows)], outs[i], osem.at[8 + i])

    def leave(i):
        result(i).start()

    def output(j):
        out = hidden_of(j) + dot(a[live_rows_of(j), :], wr[...]) + reduce_bias
        up0[j] = out.astype(bf16)

    def finish(j, carry):
        grad_normed = dot(jnp.concatenate([gj[p, live_rows_of(j), :] for p in range(PAIRS)], axis=1), wq[...], NT)
        scaled, inverse = normalise(x[j].astype(f32))
        gh[j] = gh[j] + norm_back(grad_normed, scaled, inverse, attn_gain)
        pltpu.make_async_copy(gh.at[j], grad_out.at[0, :, place(j), :], osem.at[4 + j]).start()
        return carry

    tail(finish)
    for j in range(N):
        pltpu.make_async_copy(gh.at[j], grad_out.at[0, :, place(j), :], osem.at[4 + j]).wait()
    pltpu.make_async_copy(act_t, act_out.at[0], osem.at[0]).wait()
    for i in range(len(jobs)):
        result(i).wait()


def run_main(tokens, cot, w_qkv, w_proj, w_expand, w_reduce, *rest):
    hbm = pl.BlockSpec(memory_space=pl.ANY)
    vmem = pl.BlockSpec(memory_space=pltpu.VMEM)
    smem = pl.BlockSpec(memory_space=pltpu.SMEM)
    V = pltpu.VMEM
    scratch = [
        V((N + 1, T, D), bf16), V((N, T, D), bf16), V((D, 3 * D), bf16), V((D, D), bf16), V((D, FF), bf16), V((FF, D), bf16),
        V((R, D), bf16), V((F, D), bf16), V((PAIRS, R, LANES), bf16), V((PAIRS, R + F, LANES), bf16), V((PAIRS, R + F, LANES), bf16),
        V((PAIRS, 2 * F, 2 * F), bf16), V((PAIRS * 3, 2 * F, 3 * F), bf16),
        V((PAIRS, R, LANES), bf16),
        V((3, R, D), bf16), V((R, FF), bf16), V((FF // LANES * R, LANES), bf16), V((N, T, D), f32),
        V((PAIRS, R, LANES), bf16),
        V((PAIRS, 2 * F, LANES), bf16), V((T, N, D), bf16), V((8, D), f32), V((1, FF), f32),
        pltpu.SemaphoreType.DMA((24,)), pltpu.SemaphoreType.DMA((12,)), pltpu.SemaphoreType.DMA((8,)),
    ] + Sum.scratch(FIRST, True) + Sum.scratch(LATE[0], False) + [V((LATE[1], LANES), bf16)] + Sum.scratch(LATE[1], False) + Sum.scratch(SECOND, True)
    return pl.pallas_call(
        main_kernel,
        out_shape=[
            jax.ShapeDtypeStruct((1, T, N, D), bf16), jax.ShapeDtypeStruct((1, T, N, D), f32),
            jax.ShapeDtypeStruct((EARLY, LANES), bf16), jax.ShapeDtypeStruct((LATE[0], LANES), bf16),
            jax.ShapeDtypeStruct((LATE[1], LANES), bf16),
        ],
        in_specs=[hbm] * 6 + [vmem] * 9 + [smem] * 2,
        out_specs=[hbm] * 5,
        scratch_shapes=scratch,
        compiler_params=pltpu.CompilerParams(
            collective_id=0, has_side_effects=True, vmem_limit_bytes=66_500_000
        ),
    )(tokens, cot, w_qkv, w_proj, w_expand, w_reduce, *rest)


def final_kernel(
    early_in, late0_in, late1_in, wq_in, gain_ref, shift_ref, act_in, grad_in,
    o_ag, o_as, o_wq, o_qb, o_vb, o_wp, o_pb, o_mg, o_ms, o_we, o_eb, o_wr, o_rb, o_norm, o_act, o_grad,
    early, late0, late1, wq, s_wq, s_wp, s_we, s_wr, s_act, s_grad, isem, osem,
):
    half = 12 * D
    pieces = [
        (early_in.at[pl.ds(0, half)], early.at[pl.ds(0, half)]), (early_in.at[pl.ds(half, half)], early.at[pl.ds(half, half)]),
        (early_in.at[pl.ds(2 * half, EARLY - 2 * half)], early.at[pl.ds(2 * half, EARLY - 2 * half)]),
        (late0_in, late0), (late1_in, late1), (wq_in, wq),
    ]
    whole = [pltpu.make_async_copy(act_in, s_act, isem.at[6]), pltpu.make_async_copy(grad_in, s_grad, isem.at[7])]
    for copy in whole:
        copy.start()
    fetches = [pltpu.make_async_copy(src, dst, isem.at[i]) for i, (src, dst) in enumerate(pieces)]
    for copy in fetches:
        copy.start()

    def square(total, block):
        return total + jnp.sum(block * block, axis=0, keepdims=True)

    total = jnp.zeros((1, LANES), f32)
    stores = []

    def store(src, dst):
        copy = pltpu.make_async_copy(src, dst, osem.at[len(stores)])
        copy.start()
        stores.append(copy)

    whole[0].wait()
    store(s_act, o_act)
    whole[1].wait()
    store(s_grad, o_grad)
    fetches[0].wait()
    for c in range(12):
        block = early[pl.ds(c * D, D), :].astype(f32)
        s_wr[pl.ds(c * LANES, LANES), :] = block.T
        total = square(total, block)
    store(s_wr, o_wr)
    fetches[1].wait()
    for c in range(12):
        block = early[pl.ds(half + c * D, D), :].astype(f32)
        s_we[:, pl.ds(c * LANES, LANES)] = block
        total = square(total, block)
    store(s_we, o_we)
    fetches[2].wait()
    for c in range(3):
        block = early[pl.ds(2 * half + c * D, D), :].astype(f32)
        s_wp[:, pl.ds(c * LANES, LANES)] = block
        total = square(total, block)
    store(s_wp, o_wp)
    tail = early[pl.ds(27 * D, 32), :].astype(f32)
    total = square(total, tail[:24])
    lines = [tail[i:i + 1] for i in range(24)]

    def line(parts):
        return jnp.concatenate(parts, axis=1).reshape(len(parts) * LANES)

    o_rb[...] = line(lines[:3])
    o_eb[...] = line(lines[3:15])
    o_mg[...] = line(lines[15:18])
    o_ms[...] = line(lines[18:21])
    o_pb[...] = line(lines[21:24])

    def column(ref):
        row = ref[...].reshape(1, D)
        return jnp.broadcast_to(row, (LANES, D)).T

    gain, shift = column(gain_ref), column(shift_ref)
    for copy in fetches[3:]:
        copy.wait()
    along_gain = jnp.zeros((D, LANES), f32)
    along_shift = jnp.zeros((D, LANES), f32)
    sums = {}
    for group, ref in ((0, late0), (1, late1)):
        pairs = LATES[group]
        extra = ref[pl.ds(len(pairs) * 3 * D, 16), :].astype(f32)
        for i, p in enumerate(pairs):
            for t in range(3):
                moment = ref[pl.ds((i * 3 + t) * D, D), :].astype(f32)
                summed = extra[i * 3 + t:i * 3 + t + 1]
                sums[t, p] = summed
                cols = pl.ds((t * PAIRS + p) * LANES, LANES)
                weight = wq[:, cols].astype(f32)
                block = gain * moment + shift * summed
                s_wq[:, cols] = block
                total = square(total, block)
                along_gain = along_gain + weight * moment
                along_shift = along_shift + weight * summed
    store(s_wq, o_wq)
    grad_gain = jnp.sum(along_gain.T, axis=0, keepdims=True)
    grad_shift = jnp.sum(along_shift.T, axis=0, keepdims=True)
    o_ag[...] = grad_gain.reshape(D)
    o_as[...] = grad_shift.reshape(D)
    o_qb[...] = line([sums[0, p] for p in range(PAIRS)])
    o_vb[...] = line([sums[2, p] for p in range(PAIRS)])
    for p in range(PAIRS):
        total = square(square(total, sums[0, p]), sums[2, p])
        cols = slice(p * LANES, (p + 1) * LANES)
        total = square(square(total, grad_gain[:, cols]), grad_shift[:, cols])
    o_norm[...] = jnp.sqrt(jnp.sum(total, axis=1, keepdims=True))
    for copy in stores:
        copy.wait()


def run_final(early, late0, late1, w_qkv, gain, shift, act, grad):
    hbm = pl.BlockSpec(memory_space=pl.ANY)
    vmem = pl.BlockSpec(memory_space=pltpu.VMEM)
    V = pltpu.VMEM
    vector = jax.ShapeDtypeStruct((D,), f32)

    def matrix(a, b):
        return jax.ShapeDtypeStruct((a, b), f32)

    shapes = [
        vector, vector, matrix(D, 3 * D), vector, vector, matrix(D, D), vector, vector, vector, matrix(D, FF),
        jax.ShapeDtypeStruct((FF,), f32), matrix(FF, D), vector, matrix(1, 1),
        jax.ShapeDtypeStruct(act.shape, act.dtype), jax.ShapeDtypeStruct(grad.shape, grad.dtype),
    ]
    return pl.pallas_call(
        final_kernel,
        out_shape=shapes,
        in_specs=[hbm] * 4 + [vmem] * 2 + [hbm] * 2,
        out_specs=[hbm if len(s.shape) > 1 and s.shape[-1] > 1 else vmem for s in shapes],
        scratch_shapes=[
            V((EARLY, LANES), bf16), V((LATE[0], LANES), bf16), V((LATE[1], LANES), bf16), V((D, 3 * D), bf16),
            V((D, 3 * D), f32), V((D, D), f32), V((D, FF), f32), V((FF, D), f32),
            V(act.shape, bf16), V(grad.shape, f32),
            pltpu.SemaphoreType.DMA((8,)), pltpu.SemaphoreType.DMA((6,)),
        ],
        compiler_params=pltpu.CompilerParams(vmem_limit_bytes=66_500_000),
    )(early, late0, late1, w_qkv, gain, shift, act, grad)


def body(
    tokens, attn_gain, attn_shift, w_qkv, query_bias, value_bias, w_proj, proj_bias, mlp_gain, mlp_shift,
    w_expand, expand_bias, w_reduce, reduce_bias, cotangent, resolution, frame_count,
):
    act, grad, early, late0, late1 = run_main(
        tokens, cotangent, w_qkv, w_proj, w_expand, w_reduce, attn_gain, attn_shift, query_bias, value_bias,
        proj_bias, mlp_gain, mlp_shift, reduce_bias, expand_bias, resolution, frame_count,
    )
    *grads, norm, act, grad = run_final(early, late0, late1, w_qkv, attn_gain, attn_shift, act, grad)
    return (jnp.transpose(act, (0, 2, 1, 3)), jnp.transpose(grad, (0, 2, 1, 3)), *grads, norm.reshape(()))


def solution(mesh):
    data = P("clip", "frame", None, None)
    return jax.shard_map(
        body,
        mesh=mesh,
        in_specs=(data,) + (P(),) * 13 + (data, P("clip"), P("clip")),
        out_specs=(data, data) + (P(),) * 14,
        check_vma=False,
    )
```
